32 devices in a mesh: groups: 2 (over y), tile: 4 (over z), cone: 2 (over x), rep: 2 (over core).
Axes of the slice: x: 2, y: 2, z: 4, core: 2. Of those that a mesh axis runs over, the one named last changes fastest.
Arguments:
- values: bfloat16 [1024, 6144], P(('groups', 'tile'), ('cone', 'rep')), parts along dimension 0, may hold values from -0.0546875 to 0.0546875
- pattern: int32 [8, 48], P(('groups', 'tile'), ('cone', 'rep')), parts along dimension 0, may hold values from 0 to 1, as said below
- cone_point: float32 [96, 128], P(('groups', 'cone', 'rep')), parts along dimension 0, may hold values from -1 to 2, as said below
- cone_scale: float32 [96], P(('groups', 'cone', 'rep')), parts along dimension 0, may hold values from 0.5 to 2
Outputs:
- schur: float32 [1024, 512], P(('groups', 'tile', 'cone', 'rep')), parts along dimension 0
The draws below stay inside these ranges and needn't reach their ends.
There are 2 independent parts, one for each index of `groups`. The reference program is written for one: setup_inputs(seed, part) draws one part's arguments, and reference() takes and returns one part's arrays. A program takes and returns all parts, laid end to end along the dimension named above; each array names one. Nothing has to cross between parts.
Inputs may be any that keep to these rules, and one draw needn't show every extreme that they name: `pattern`: entries are 0 or 1. Among the 12 tiles of one row block in one column group (columns of 12 consecutive cones starting at a multiple of 12) at least 1 and at most 6 are 1; every row block has exactly 6 in some column group. `cone_point`: in every row the first entry is larger than the Euclidean length of the other entries by a margin, so det stays at 0.19 or more.
All inputs are finite; a program needn't handle non-finite values.
Results may differ from the reference program's by a relative error of at most 0.0018.
Values may be sent and summed in bfloat16 or wider, within the bound.
A program may use at most 64 MiB of HBM per device.

```python
import math
import jax
import jax.numpy as jnp
from jax import lax

CONE = 128
CT_DEV = 12
NZ_MOST = 6
CONES = 48
COLS = 6144
ROWS = 512
N_TILE = 4
N_CONE = 2
N_REP = 2


def draw_pattern(key, part):
    key = jax.random.fold_in(key, 11)
    first, second = jax.random.split(key)
    column_groups = N_CONE * N_REP
    counts = jax.random.randint(first, (N_TILE, column_groups), 1, NZ_MOST + 1)
    forced = jnp.arange(column_groups)[None, :] == jnp.arange(N_TILE)[:, None] % column_groups
    counts = jnp.where(forced, NZ_MOST, counts)
    scores = jax.random.randint(second, (N_TILE, column_groups, CT_DEV), 0, 1 << 20) * CT_DEV + jnp.arange(CT_DEV)[None, None, :]
    ranks = jnp.argsort(jnp.argsort(scores, axis=-1), axis=-1)
    return (ranks < counts[:, :, None]).astype(jnp.int32).reshape(N_TILE, CONES)


def draw_cone_point(key, part):
    key = jax.random.fold_in(key, 5)
    first, second = jax.random.split(key)
    reach = 0.9 / math.sqrt(CONE - 1)
    head = jax.random.uniform(first, (CONES, 1), jnp.float32, 1.2, 2.0)
    tail = jax.random.uniform(second, (CONES, CONE - 1), jnp.float32, -reach, reach)
    return jnp.concatenate([head, tail], axis=1).astype(jnp.float32)


def block_scale(stream_key, extent, pieces, smallest, high):
    def one(dim, parts):
        heights = jax.random.uniform(jax.random.fold_in(jax.random.fold_in(stream_key, 6), dim), (parts,), jnp.float32, smallest / len(pieces), high / len(pieces))
        return jnp.repeat(jnp.exp(heights), extent[dim] // parts).reshape((-1,) + (1,) * (len(extent) - dim - 1))

    level = one(*pieces[0])
    for cut in pieces[1:]:
        level = level * one(*cut)
    return level


def gaussian(rng, dims, width, most, cuts=(), held_as=jnp.bfloat16):
    entries = jax.random.normal(rng, dims, jnp.float32) * width
    if len(cuts) > 0:
        entries = block_scale(rng, dims, cuts, -0.22, 0.18) * entries
    return jnp.clip(entries, min=-most, max=most).astype(held_as)


def setup_inputs(seed: int = 0, part: int = 0) -> dict:
    key_list = jax.random.split(jax.random.key(seed), 5)
    part_splits = jax.random.split(jax.random.fold_in(key_list[4], part), 5)
    values = gaussian(part_splits[0], (ROWS, COLS), (2 * COLS) ** -0.5, 0.0546875, ((0, 4), (1, 4)))
    pattern = draw_pattern(jax.random.fold_in(jax.random.fold_in(key_list[4], part), 71), part)
    cone_point = draw_cone_point(jax.random.fold_in(jax.random.fold_in(key_list[4], part), 71), part)
    cone_scale = jnp.clip(jnp.exp(math.log(2.0) - 1.3862944 * jax.random.uniform(part_splits[3], (CONES,), jnp.float32) ** block_scale(part_splits[3], (CONES,), ((0, 4),), -0.2, 0.2)), 0.5, 2.0)
    return {"values": values, "pattern": pattern, "cone_point": cone_point, "cone_scale": cone_scale}


def reference(values, pattern, cone_point, cone_scale):
    rows, cols = values.shape
    row_tiles = rows // CONE
    cones = cols // CONE
    live = pattern.astype(jnp.bfloat16)
    masked = (values.reshape(row_tiles, CONE, cones, CONE) * live[:, None, :, None]).reshape(rows, cols)
    head = cone_point[:, 0]
    tail = cone_point[:, 1:]
    det = head * head - lax.optimization_barrier(jnp.sum(tail * tail, axis=1))
    unit = cone_point / jnp.sqrt(det)[:, None]
    signs = jnp.where(jnp.arange(CONE) == 0, 1.0, -1.0).astype(jnp.float32)
    blocks = masked.astype(jnp.float32).reshape(rows, cones, CONE)
    proj = jnp.einsum('rkc,kc->rk', blocks, unit, precision=lax.Precision.HIGHEST)
    factor = cone_scale[None, :, None]
    scaled = (factor * (2.0 * proj[:, :, None] * unit[None, :, :] - blocks * signs[None, None, :])).astype(jnp.bfloat16)
    scaled = scaled.reshape(rows, cols)
    return lax.dot_general(scaled, scaled, (((1,), (1,)), ((), ())), preferred_element_type=jnp.float32)
```

```python
import functools

import jax
import jax.numpy as jnp
from jax import lax
from jax.experimental import pallas as pl
from jax.experimental.pallas import tpu as pltpu
from jax.sharding import PartitionSpec as P

MESH = pl.DeviceIdType.MESH
SLOTS = 6


def kernel(n_tile, n_cone, n_rep, pattern_ref, scale_ref, values_ref, point_ref, out_ref,
           unit_ref, held, ids, part, landed, send_sem, recv_sem, part_send, part_recv):
    rows = values_ref.shape[0]
    cones, width = point_ref.shape
    n_sum = n_cone * n_rep
    strip = rows // n_sum
    me = lax.axis_index("tile")
    here = lax.axis_index("cone") * n_rep + lax.axis_index("rep")
    has_left, has_right = me > 0, me < n_tile - 1

    def peer(d):
        other = lax.rem(here + d, n_sum)
        return other, {"cone": other // n_rep, "rep": lax.rem(other, n_rep)}

    barrier = pltpu.get_barrier_semaphore()

    @pl.when(has_left)
    def _():
        pl.semaphore_signal(barrier, inc=1, device_id={"tile": me - 1}, device_id_type=MESH)

    @pl.when(has_right)
    def _():
        pl.semaphore_signal(barrier, inc=1, device_id={"tile": me + 1}, device_id_type=MESH)

    for d in range(1, n_sum):
        pl.semaphore_signal(barrier, inc=1, device_id=peer(d)[1], device_id_type=MESH)

    chosen = [[] for _ in range(SLOTS)]
    count = jnp.int32(0)
    for k in range(cones):
        live = pattern_ref[0, k]
        for s in range(SLOTS):
            chosen[s].append(live * (count == s).astype(jnp.int32) if k >= s else None)
        count = count + live
    for s in range(SLOTS):
        name = sum(chosen[s][k] * (k + 1) for k in range(s, cones))
        ids[me, s : s + 1, :] = jnp.full((1, width), name, jnp.int32)

    lane = lax.broadcasted_iota(jnp.int32, (1, width), 1)
    signs = jnp.where(lane == 0, 1.0, -1.0).astype(jnp.float32)
    point = point_ref[...]
    det = jnp.sum(point * point * signs, axis=1, keepdims=True)
    unit_ref[...] = point / jnp.sqrt(det)

    def block_copy(src, piece, right):
        ref = ids.at[src] if piece == SLOTS else held.at[src, piece]
        return pltpu.make_async_remote_copy(
            src_ref=ref,
            dst_ref=ref,
            send_sem=send_sem.at[0 if right else 1, src, piece],
            recv_sem=recv_sem.at[src, piece],
            device_id={"tile": me + 1 if right else me - 1},
            device_id_type=MESH,
        )

    def send_own(piece):
        @pl.when(has_right)
        def _():
            block_copy(me, piece, True).start()

        @pl.when(has_left)
        def _():
            block_copy(me, piece, False).start()

    pl.semaphore_wait(
        barrier, has_left.astype(jnp.int32) + has_right.astype(jnp.int32) + (n_sum - 1)
    )
    send_own(SLOTS)
    for s in range(SLOTS):
        factor, unit, packed = 0.0, 0.0, None
        for k in range(s, cones):
            weight = chosen[s][k].astype(jnp.float32)
            factor = factor + weight * scale_ref[k]
            unit = unit + weight * unit_ref[k : k + 1, :]
            mask = jnp.full((1, width), weight, jnp.float32).astype(jnp.bfloat16)
            term = values_ref[:, k * width : (k + 1) * width] * mask
            packed = term if packed is None else packed + term
        tile = packed.astype(jnp.float32)
        proj = jnp.sum(tile * unit, axis=1, keepdims=True)
        held[me, s] = (factor * (2.0 * proj * unit - tile * signs)).astype(jnp.bfloat16)
        send_own(s)

    def part_copy(src, d):
        other, device = peer(d)
        return pltpu.make_async_remote_copy(
            src_ref=part.at[src, other],
            dst_ref=landed.at[src, d - 1],
            send_sem=part_send.at[src, d - 1],
            recv_sem=part_recv.at[src, d - 1],
            device_id=device,
            device_id_type=MESH,
        )

    def product(src, own):
        mine = [held[me, s] for s in range(SLOTS)]
        if own:
            left = mine
        else:
            left = []
            for b in range(SLOTS):
                total = None
                for a in range(SLOTS):
                    same = (ids[me, a : a + 1, :] == ids[src, b : b + 1, :]).astype(jnp.float32)
                    term = mine[a] * same.astype(jnp.bfloat16)
                    total = term if total is None else total + term
                left.append(total)
        block = lax.dot_general(
            jnp.concatenate(left, axis=1),
            jnp.concatenate([held[src, s] for s in range(SLOTS)], axis=1),
            (((1,), (1,)), ((), ())),
            preferred_element_type=jnp.float32,
        )
        part[src] = block.reshape(n_sum, strip, width)
        for d in range(1, n_sum):
            part_copy(src, d).start()

    product(me, True)

    def step(s, carry):
        from_left, from_right = me - s, me + s
        for piece in (SLOTS, *range(SLOTS)):
            @pl.when(from_left >= 0)
            def _():
                block_copy(from_left, piece, True).wait_recv()

                @pl.when(has_right)
                def _():
                    block_copy(from_left, piece, True).start()

            @pl.when(from_right < n_tile)
            def _():
                block_copy(from_right, piece, False).wait_recv()

                @pl.when(has_left)
                def _():
                    block_copy(from_right, piece, False).start()

        @pl.when(from_left >= 0)
        def _():
            product(from_left, False)

        @pl.when(from_right < n_tile)
        def _():
            product(from_right, False)

        return carry

    lax.fori_loop(1, n_tile, step, 0)

    for src in range(n_tile):
        total = part[src, here]
        for d in range(1, n_sum):
            part_copy(src, d).wait_recv()
            total = total + landed[src, d - 1]
        out_ref[:, src * rows : (src + 1) * rows] = total

    def drain(src, carry):
        for d in range(1, n_sum):
            part_copy(src, d).wait_send()

        @pl.when(jnp.logical_and(has_right, src <= me))
        def _():
            for piece in range(SLOTS + 1):
                block_copy(src, piece, True).wait_send()

        @pl.when(jnp.logical_and(has_left, src >= me))
        def _():
            for piece in range(SLOTS + 1):
                block_copy(src, piece, False).wait_send()

        return carry

    lax.fori_loop(0, n_tile, drain, 0)


def solution(mesh):
    n_tile, n_cone, n_rep = mesh.shape["tile"], mesh.shape["cone"], mesh.shape["rep"]
    n_sum = n_cone * n_rep

    def per_device(values, pattern, cone_point, cone_scale):
        rows, cols = values.shape
        cones, width = cone_point.shape
        strip = rows // n_sum
        vmem = pl.BlockSpec(memory_space=pltpu.VMEM)
        smem = pl.BlockSpec(memory_space=pltpu.SMEM)
        return pl.pallas_call(
            functools.partial(kernel, n_tile, n_cone, n_rep),
            out_shape=jax.ShapeDtypeStruct((strip, n_tile * rows), jnp.float32),
            in_specs=[smem, smem, vmem, vmem],
            out_specs=vmem,
            scratch_shapes=[
                pltpu.VMEM((cones, width), jnp.float32),
                pltpu.VMEM((n_tile, SLOTS, rows, width), jnp.bfloat16),
                pltpu.VMEM((n_tile, 8, width), jnp.int32),
                pltpu.VMEM((n_tile, n_sum, strip, rows), jnp.float32),
                pltpu.VMEM((n_tile, n_sum - 1, strip, rows), jnp.float32),
                pltpu.SemaphoreType.DMA((2, n_tile, SLOTS + 1)),
                pltpu.SemaphoreType.DMA((n_tile, SLOTS + 1)),
                pltpu.SemaphoreType.DMA((n_tile, n_sum - 1)),
                pltpu.SemaphoreType.DMA((n_tile, n_sum - 1)),
            ],
            compiler_params=pltpu.CompilerParams(
                collective_id=0, has_side_effects=True, vmem_limit_bytes=32 * 1024 * 1024
            ),
        )(pattern, cone_scale, values, cone_point)

    return jax.shard_map(
        per_device,
        mesh=mesh,
        in_specs=(
            P(("groups", "tile"), ("cone", "rep")),
            P(("groups", "tile"), ("cone", "rep")),
            P(("groups", "cone", "rep"), None),
            P(("groups", "cone", "rep")),
        ),
        out_specs=P(("groups", "tile", "cone", "rep"), None),
        check_vma=False,
    )
```

```python
import functools

import jax
import jax.numpy as jnp
from jax import lax
from jax.experimental import pallas as pl
from jax.experimental.pallas import tpu as pltpu
from jax.sharding import PartitionSpec as P

MESH = pl.DeviceIdType.MESH
SLOTS = 6


def kernel(n_tile, n_cone, n_rep, pattern_hbm, scale_hbm, values_hbm, point_hbm, out_ref,
           pattern_ref, scale_ref, values_ref, point_ref, load_sem, unit_ref, held, ids, part, landed, send_sem, recv_sem, part_send, part_recv):
    rows = values_ref.shape[0]
    cones, width = point_ref.shape
    n_sum = n_cone * n_rep
    strip = rows // n_sum
    me = lax.axis_index("tile")
    here = lax.axis_index("cone") * n_rep + lax.axis_index("rep")
    has_left, has_right = me > 0, me < n_tile - 1

    def peer(d):
        other = lax.rem(here + d, n_sum)
        return other, {"cone": other // n_rep, "rep": lax.rem(other, n_rep)}

    barrier = pltpu.get_barrier_semaphore()

    @pl.when(has_left)
    def _():
        pl.semaphore_signal(barrier, inc=1, device_id={"tile": me - 1}, device_id_type=MESH)

    @pl.when(has_right)
    def _():
        pl.semaphore_signal(barrier, inc=1, device_id={"tile": me + 1}, device_id_type=MESH)

    for d in range(1, n_sum):
        pl.semaphore_signal(barrier, inc=1, device_id=peer(d)[1], device_id_type=MESH)

    loads = [
        pltpu.make_async_copy(src, dst, load_sem.at[i])
        for i, (src, dst) in enumerate(
            (
                (pattern_hbm, pattern_ref),
                (scale_hbm, scale_ref),
                (point_hbm, point_ref),
                (values_hbm, values_ref),
            )
        )
    ]
    for load in loads:
        load.start()
    loads[0].wait()

    chosen = [[] for _ in range(SLOTS)]
    count = jnp.int32(0)
    for k in range(cones):
        live = pattern_ref[0, k]
        for s in range(SLOTS):
            chosen[s].append(live * (count == s).astype(jnp.int32) if k >= s else None)
        count = count + live
    for s in range(SLOTS):
        name = sum(chosen[s][k] * (k + 1) for k in range(s, cones))
        ids[me, s : s + 1, :] = jnp.full((1, width), name, jnp.int32)

    lane = lax.broadcasted_iota(jnp.int32, (1, width), 1)
    signs = jnp.where(lane == 0, 1.0, -1.0).astype(jnp.float32)
    loads[2].wait()
    point = point_ref[...]
    det = jnp.sum(point * point * signs, axis=1, keepdims=True)
    unit_ref[...] = point / jnp.sqrt(det)

    def block_copy(src, piece, right):
        ref = ids.at[src] if piece == SLOTS else held.at[src, piece]
        return pltpu.make_async_remote_copy(
            src_ref=ref,
            dst_ref=ref,
            send_sem=send_sem.at[0 if right else 1, src, piece],
            recv_sem=recv_sem.at[src, piece],
            device_id={"tile": me + 1 if right else me - 1},
            device_id_type=MESH,
        )

    def send_own(piece):
        @pl.when(has_right)
        def _():
            block_copy(me, piece, True).start()

        @pl.when(has_left)
        def _():
            block_copy(me, piece, False).start()

    pl.semaphore_wait(
        barrier, has_left.astype(jnp.int32) + has_right.astype(jnp.int32) + (n_sum - 1)
    )
    send_own(SLOTS)
    loads[1].wait()
    loads[3].wait()
    for s in range(SLOTS):
        factor, unit, packed = 0.0, 0.0, None
        for k in range(s, cones):
            weight = chosen[s][k].astype(jnp.float32)
            factor = factor + weight * scale_ref[k]
            unit = unit + weight * unit_ref[k : k + 1, :]
            mask = jnp.full((1, width), weight, jnp.float32).astype(jnp.bfloat16)
            term = values_ref[:, k * width : (k + 1) * width] * mask
            packed = term if packed is None else packed + term
        tile = packed.astype(jnp.float32)
        proj = jnp.sum(tile * unit, axis=1, keepdims=True)
        held[me, s] = (factor * (2.0 * proj * unit - tile * signs)).astype(jnp.bfloat16)
        send_own(s)

    def part_copy(src, d):
        other, device = peer(d)
        return pltpu.make_async_remote_copy(
            src_ref=part.at[src, other],
            dst_ref=landed.at[src, d - 1],
            send_sem=part_send.at[src, d - 1],
            recv_sem=part_recv.at[src, d - 1],
            device_id=device,
            device_id_type=MESH,
        )

    def product(src, own):
        mine = [held[me, s] for s in range(SLOTS)]
        if own:
            left = mine
        else:
            left = []
            for b in range(SLOTS):
                total = None
                for a in range(SLOTS):
                    same = (ids[me, a : a + 1, :] == ids[src, b : b + 1, :]).astype(jnp.float32)
                    term = mine[a] * same.astype(jnp.bfloat16)
                    total = term if total is None else total + term
                left.append(total)
        block = lax.dot_general(
            jnp.concatenate(left, axis=1),
            jnp.concatenate([held[src, s] for s in range(SLOTS)], axis=1),
            (((1,), (1,)), ((), ())),
            preferred_element_type=jnp.float32,
        )
        part[src] = block.reshape(n_sum, strip, width)
        for d in range(1, n_sum):
            part_copy(src, d).start()

    product(me, True)

    def step(s, carry):
        from_left, from_right = me - s, me + s
        for piece in (SLOTS, *range(SLOTS)):
            @pl.when(from_left >= 0)
            def _():
                block_copy(from_left, piece, True).wait_recv()

                @pl.when(has_right)
                def _():
                    block_copy(from_left, piece, True).start()

            @pl.when(from_right < n_tile)
            def _():
                block_copy(from_right, piece, False).wait_recv()

                @pl.when(has_left)
                def _():
                    block_copy(from_right, piece, False).start()

        @pl.when(from_left >= 0)
        def _():
            product(from_left, False)

        @pl.when(from_right < n_tile)
        def _():
            product(from_right, False)

        return carry

    lax.fori_loop(1, n_tile, step, 0)

    for src in range(n_tile):
        total = part[src, here]
        for d in range(1, n_sum):
            part_copy(src, d).wait_recv()
            total = total + landed[src, d - 1]
        out_ref[:, src * rows : (src + 1) * rows] = total

    def drain(src, carry):
        for d in range(1, n_sum):
            part_copy(src, d).wait_send()

        @pl.when(jnp.logical_and(has_right, src <= me))
        def _():
            for piece in range(SLOTS + 1):
                block_copy(src, piece, True).wait_send()

        @pl.when(jnp.logical_and(has_left, src >= me))
        def _():
            for piece in range(SLOTS + 1):
                block_copy(src, piece, False).wait_send()

        return carry

    lax.fori_loop(0, n_tile, drain, 0)


def solution(mesh):
    n_tile, n_cone, n_rep = mesh.shape["tile"], mesh.shape["cone"], mesh.shape["rep"]
    n_sum = n_cone * n_rep

    def per_device(values, pattern, cone_point, cone_scale):
        rows, cols = values.shape
        cones, width = cone_point.shape
        strip = rows // n_sum
        vmem = pl.BlockSpec(memory_space=pltpu.VMEM)
        hbm = pl.BlockSpec(memory_space=pltpu.HBM)
        return pl.pallas_call(
            functools.partial(kernel, n_tile, n_cone, n_rep),
            out_shape=jax.ShapeDtypeStruct((strip, n_tile * rows), jnp.float32),
            in_specs=[hbm] * 4,
            out_specs=vmem,
            scratch_shapes=[
                pltpu.SMEM(pattern.shape, jnp.int32),
                pltpu.SMEM(cone_scale.shape, jnp.float32),
                pltpu.VMEM(values.shape, jnp.bfloat16),
                pltpu.VMEM((cones, width), jnp.float32),
                pltpu.SemaphoreType.DMA((4,)),
                pltpu.VMEM((cones, width), jnp.float32),
                pltpu.VMEM((n_tile, SLOTS, rows, width), jnp.bfloat16),
                pltpu.VMEM((n_tile, 8, width), jnp.int32),
                pltpu.VMEM((n_tile, n_sum, strip, rows), jnp.float32),
                pltpu.VMEM((n_tile, n_sum - 1, strip, rows), jnp.float32),
                pltpu.SemaphoreType.DMA((2, n_tile, SLOTS + 1)),
                pltpu.SemaphoreType.DMA((n_tile, SLOTS + 1)),
                pltpu.SemaphoreType.DMA((n_tile, n_sum - 1)),
                pltpu.SemaphoreType.DMA((n_tile, n_sum - 1)),
            ],
            compiler_params=pltpu.CompilerParams(
                collective_id=0, has_side_effects=True, vmem_limit_bytes=32 * 1024 * 1024
            ),
        )(pattern, cone_scale, values, cone_point)

    return jax.shard_map(
        per_device,
        mesh=mesh,
        in_specs=(
            P(("groups", "tile"), ("cone", "rep")),
            P(("groups", "tile"), ("cone", "rep")),
            P(("groups", "cone", "rep"), None),
            P(("groups", "cone", "rep")),
        ),
        out_specs=P(("groups", "tile", "cone", "rep"), None),
        check_vma=False,
    )
```

```python
import functools

import jax
import jax.numpy as jnp
from jax import lax
from jax.experimental import pallas as pl
from jax.experimental.pallas import tpu as pltpu
from jax.sharding import PartitionSpec as P

MESH = pl.DeviceIdType.MESH
SLOTS = 6


def kernel(n_tile, n_cone, n_rep, pattern_hbm, scale_hbm, values_hbm, point_hbm, out_ref,
           pattern_ref, scale_ref, values_ref, point_ref, load_sem, unit_ref, held, ids, part, landed, send_sem, recv_sem, part_send, part_recv):
    rows = values_ref.shape[0]
    cones, width = point_ref.shape
    n_sum = n_cone * n_rep
    strip = rows // n_sum
    me = lax.axis_index("tile")
    here = lax.axis_index("cone") * n_rep + lax.axis_index("rep")
    has_left, has_right = me > 0, me < n_tile - 1

    def peer(d):
        other = lax.rem(here + d, n_sum)
        return other, {"cone": other // n_rep, "rep": lax.rem(other, n_rep)}

    barrier = pltpu.get_barrier_semaphore()

    @pl.when(has_left)
    def _():
        pl.semaphore_signal(barrier, inc=1, device_id={"tile": me - 1}, device_id_type=MESH)

    @pl.when(has_right)
    def _():
        pl.semaphore_signal(barrier, inc=1, device_id={"tile": me + 1}, device_id_type=MESH)

    for d in range(1, n_sum):
        pl.semaphore_signal(barrier, inc=1, device_id=peer(d)[1], device_id_type=MESH)

    loads = [
        pltpu.make_async_copy(src, dst, load_sem.at[i])
        for i, (src, dst) in enumerate(
            (
                (pattern_hbm, pattern_ref),
                (scale_hbm, scale_ref),
                (point_hbm, point_ref),
                (values_hbm, values_ref),
            )
        )
    ]
    for load in loads:
        load.start()
    loads[0].wait()

    chosen = [[] for _ in range(SLOTS)]
    count = jnp.int32(0)
    for k in range(cones):
        live = pattern_ref[0, k]
        for s in range(SLOTS):
            chosen[s].append(live * (count == s).astype(jnp.int32) if k >= s else None)
        count = count + live
    for s in range(SLOTS):
        name = sum(chosen[s][k] * (k + 1) for k in range(s, cones))
        ids[me, s : s + 1, :] = jnp.full((1, width), name, jnp.int32)

    lane = lax.broadcasted_iota(jnp.int32, (1, width), 1)
    signs = jnp.where(lane == 0, 1.0, -1.0).astype(jnp.float32)
    loads[2].wait()
    point = point_ref[...]
    det = jnp.sum(point * point * signs, axis=1, keepdims=True)
    unit_ref[...] = point / jnp.sqrt(det)

    def block_copy(src, piece, right):
        ref = ids.at[src] if piece == SLOTS else held.at[src, piece]
        return pltpu.make_async_remote_copy(
            src_ref=ref,
            dst_ref=ref,
            send_sem=send_sem.at[0 if right else 1, src, piece],
            recv_sem=recv_sem.at[src, piece],
            device_id={"tile": me + 1 if right else me - 1},
            device_id_type=MESH,
        )

    def send_own(piece):
        @pl.when(has_right)
        def _():
            block_copy(me, piece, True).start()

        @pl.when(has_left)
        def _():
            block_copy(me, piece, False).start()

    pl.semaphore_wait(
        barrier, has_left.astype(jnp.int32) + has_right.astype(jnp.int32) + (n_sum - 1)
    )
    send_own(SLOTS)
    loads[1].wait()
    loads[3].wait()
    for s in range(SLOTS):
        factor, unit, packed = 0.0, 0.0, None
        for k in range(s, cones):
            weight = chosen[s][k].astype(jnp.float32)
            factor = factor + weight * scale_ref[k]
            unit = unit + weight * unit_ref[k : k + 1, :]
            mask = jnp.full((1, width), weight, jnp.float32).astype(jnp.bfloat16)
            term = values_ref[:, k * width : (k + 1) * width] * mask
            packed = term if packed is None else packed + term
        tile = packed.astype(jnp.float32)
        proj = jnp.sum(tile * unit, axis=1, keepdims=True)
        held[me, s] = (factor * (2.0 * proj * unit - tile * signs)).astype(jnp.bfloat16)
        send_own(s)

    def part_copy(src, d):
        other, device = peer(d)
        return pltpu.make_async_remote_copy(
            src_ref=part.at[src, other],
            dst_ref=landed.at[src, d - 1],
            send_sem=part_send.at[src, d - 1],
            recv_sem=part_recv.at[src, d - 1],
            device_id=device,
            device_id_type=MESH,
        )

    def product(src, own):
        mine = [held[me, s] for s in range(SLOTS)]
        if own:
            left = mine
        else:
            left = []
            for b in range(SLOTS):
                total = None
                for a in range(SLOTS):
                    same = (ids[me, a : a + 1, :] == ids[src, b : b + 1, :]).astype(jnp.float32)
                    term = mine[a] * same.astype(jnp.bfloat16)
                    total = term if total is None else total + term
                left.append(total)
        block = lax.dot_general(
            jnp.concatenate(left, axis=1),
            jnp.concatenate([held[src, s] for s in range(SLOTS)], axis=1),
            (((1,), (1,)), ((), ())),
            preferred_element_type=jnp.float32,
        )
        part[src] = block.reshape(n_sum, strip, width)
        for d in range(1, n_sum):
            part_copy(src, d).start()

    product(me, True)

    def step(s, carry):
        from_left, from_right = me - s, me + s
        for piece in (SLOTS, *range(SLOTS)):
            @pl.when(from_left >= 0)
            def _():
                block_copy(from_left, piece, True).wait_recv()

                @pl.when(has_right)
                def _():
                    block_copy(from_left, piece, True).start()

            @pl.when(from_right < n_tile)
            def _():
                block_copy(from_right, piece, False).wait_recv()

                @pl.when(has_left)
                def _():
                    block_copy(from_right, piece, False).start()

        @pl.when(from_left >= 0)
        def _():
            product(from_left, False)

        @pl.when(from_right < n_tile)
        def _():
            product(from_right, False)

        return carry

    lax.fori_loop(1, n_tile, step, 0)

    for src in range(n_tile):
        total = part[src, here]
        for d in range(1, n_sum):
            part_copy(src, d).wait_recv()
            total = total + landed[src, d - 1]
        out_ref[:, src * rows : (src + 1) * rows] = total

    def drain(src, carry):
        for d in range(1, n_sum):
            part_copy(src, d).wait_send()

        @pl.when(jnp.logical_and(has_right, src <= me))
        def _():
            for piece in range(SLOTS + 1):
                block_copy(src, piece, True).wait_send()

        @pl.when(jnp.logical_and(has_left, src >= me))
        def _():
            for piece in range(SLOTS + 1):
                block_copy(src, piece, False).wait_send()

        return carry

    lax.fori_loop(0, n_tile, drain, 0)


def solution(mesh):
    n_tile, n_cone, n_rep = mesh.shape["tile"], mesh.shape["cone"], mesh.shape["rep"]
    n_sum = n_cone * n_rep

    def per_device(values, pattern, cone_point, cone_scale):
        rows, cols = values.shape
        cones, width = cone_point.shape
        strip = rows // n_sum
        vmem = pl.BlockSpec(memory_space=pltpu.VMEM)
        hbm = pl.BlockSpec(memory_space=pltpu.HBM)
        return pl.pallas_call(
            functools.partial(kernel, n_tile, n_cone, n_rep),
            out_shape=jax.ShapeDtypeStruct((strip, n_tile * rows), jnp.float32),
            in_specs=[hbm] * 4,
            out_specs=vmem,
            scratch_shapes=[
                pltpu.SMEM(pattern.shape, jnp.int32),
                pltpu.SMEM(cone_scale.shape, jnp.float32),
                pltpu.VMEM(values.shape, jnp.bfloat16),
                pltpu.VMEM((cones, width), jnp.float32),
                pltpu.SemaphoreType.DMA((4,)),
                pltpu.VMEM((cones, width), jnp.float32),
                pltpu.VMEM((n_tile, SLOTS, rows, width), jnp.bfloat16),
                pltpu.VMEM((n_tile, 8, width), jnp.int32),
                pltpu.VMEM((n_tile, n_sum, strip, rows), jnp.float32),
                pltpu.VMEM((n_tile, n_sum - 1, strip, rows), jnp.float32),
                pltpu.SemaphoreType.DMA((2, n_tile, SLOTS + 1)),
                pltpu.SemaphoreType.DMA((n_tile, SLOTS + 1)),
                pltpu.SemaphoreType.DMA((n_tile, n_sum - 1)),
                pltpu.SemaphoreType.DMA((n_tile, n_sum - 1)),
            ],
            compiler_params=pltpu.CompilerParams(
                collective_id=0, has_side_effects=True, vmem_limit_bytes=60 * 1024 * 1024
            ),
        )(pattern, cone_scale, values, cone_point)

    return jax.shard_map(
        per_device,
        mesh=mesh,
        in_specs=(
            P(("groups", "tile"), ("cone", "rep")),
            P(("groups", "tile"), ("cone", "rep")),
            P(("groups", "cone", "rep"), None),
            P(("groups", "cone", "rep")),
        ),
        out_specs=P(("groups", "tile", "cone", "rep"), None),
        check_vma=False,
    )
```

```python
import functools

import jax
import jax.numpy as jnp
from jax import lax
from jax.experimental import pallas as pl
from jax.experimental.pallas import tpu as pltpu
from jax.sharding import PartitionSpec as P

MESH = pl.DeviceIdType.MESH
SLOTS = 6


PARTIAL = jnp.float32


def pack(pattern_ref, scale_ref, values_ref, point_ref, unit_ref, ids_me, held_me, waits, on_ids, on_slot):
    cones, width = point_ref.shape
    waits[0]()
    chosen = [[] for _ in range(SLOTS)]
    count = jnp.int32(0)
    for k in range(cones):
        live = pattern_ref[0, k]
        for s in range(SLOTS):
            chosen[s].append(live * (count == s).astype(jnp.int32) if k >= s else None)
        count = count + live
    for s in range(SLOTS):
        name = sum(chosen[s][k] * (k + 1) for k in range(s, cones))
        ids_me[s : s + 1, :] = jnp.full((1, width), name, jnp.int32)
    on_ids()
    waits[2]()
    lane = lax.broadcasted_iota(jnp.int32, (1, width), 1)
    signs = jnp.where(lane == 0, 1.0, -1.0).astype(jnp.float32)
    point = point_ref[...]
    det = jnp.sum(point * point * signs, axis=1, keepdims=True)
    unit_ref[...] = point / jnp.sqrt(det)
    waits[1]()
    waits[3]()
    for s in range(SLOTS):
        factor, unit, packed = 0.0, 0.0, None
        for k in range(s, cones):
            weight = chosen[s][k].astype(jnp.float32)
            factor = factor + weight * scale_ref[k]
            unit = unit + weight * unit_ref[k : k + 1, :]
            mask = jnp.full((1, width), weight, jnp.float32).astype(jnp.bfloat16)
            term = values_ref[:, k * width : (k + 1) * width] * mask
            packed = term if packed is None else packed + term
        tile = packed.astype(jnp.float32)
        proj = jnp.sum(tile * unit, axis=1, keepdims=True)
        held_me[s] = (factor * (2.0 * proj * unit - tile * signs)).astype(jnp.bfloat16)
        on_slot(s)


def load_all(pairs, load_sem):
    loads = [
        pltpu.make_async_copy(src, dst, load_sem.at[i]) for i, (src, dst) in enumerate(pairs)
    ]
    for load in loads:
        load.start()
    return [load.wait for load in loads]


def matched(first, first_ids, second_ids):
    moved = []
    for b in range(SLOTS):
        total = None
        for a in range(SLOTS):
            same = (first_ids[a : a + 1, :] == second_ids[b : b + 1, :]).astype(jnp.float32)
            term = first[a] * same.astype(jnp.bfloat16)
            total = term if total is None else total + term
        moved.append(total)
    return jnp.concatenate(moved, axis=1)


def wide(ref):
    return jnp.concatenate([ref[s] for s in range(SLOTS)], axis=1)


def outer(x, y):
    return lax.dot_general(
        x, y, (((1,), (1,)), ((), ())), preferred_element_type=jnp.float32
    )


def middle_kernel(n_cone, n_rep, pattern_hbm, scale_hbm, values_hbm, point_hbm, out_ref,
                  pattern_ref, scale_ref, values_ref, point_ref, load_sem, unit_ref, held, ids,
                  own, part, landed, send_sem, recv_sem, part_send, part_recv):
    n_tile = 4
    rows, width = values_ref.shape[0], point_ref.shape[1]
    n_sum = n_cone * n_rep
    strip = rows // n_sum
    me, rep = lax.axis_index("tile"), lax.axis_index("rep")
    here = lax.axis_index("cone") * n_rep + rep
    middle = jnp.logical_or(me == 1, me == 2)
    end = jnp.logical_not(middle)
    twin = n_tile - 1 - me
    near = jnp.where(me < 2, 0, 3)
    far = 3 - near
    heavy = jnp.logical_and(middle, (me == 1) == (rep == 0))
    light = jnp.logical_and(middle, (me == 1) != (rep == 0))

    def place(tile, group):
        return {"tile": tile, "cone": group // n_rep, "rep": lax.rem(group, n_rep)}

    barrier = pltpu.get_barrier_semaphore()
    everyone = n_tile * n_sum
    for d in range(1, everyone):
        other = lax.rem(me * n_sum + here + d, everyone)
        pl.semaphore_signal(
            barrier, inc=1, device_id=place(other // n_sum, lax.rem(other, n_sum)), device_id_type=MESH
        )
    waits = load_all(
        (
            (pattern_hbm, pattern_ref),
            (scale_hbm, scale_ref),
            (point_hbm, point_ref),
            (values_hbm, values_ref),
        ),
        load_sem,
    )

    def block_copy(src, piece):
        ref = ids.at[src] if piece == SLOTS else held.at[src, piece]
        return pltpu.make_async_remote_copy(
            src_ref=ref,
            dst_ref=ref,
            send_sem=send_sem.at[src, piece],
            recv_sem=recv_sem.at[src, piece],
            device_id={"tile": jnp.where(middle, twin, jnp.where(me == 0, 1, 2))},
            device_id_type=MESH,
        )

    def send_own(piece):
        @pl.when(jnp.logical_not(heavy))
        def _():
            block_copy(me, piece).start()

    def on_ids():
        pl.semaphore_wait(barrier, everyone - 1)
        send_own(SLOTS)

    pack(pattern_ref, scale_ref, values_ref, point_ref, unit_ref, ids.at[me], held.at[me], waits, on_ids, send_own)

    def strip_copy(slot, x, y, d):
        group = lax.rem(here + d, n_sum)
        return pltpu.make_async_remote_copy(
            src_ref=part.at[slot, group],
            dst_ref=landed.at[y, here],
            send_sem=part_send.at[slot, group],
            recv_sem=part_recv.at[y, here],
            device_id=place(x, group),
            device_id_type=MESH,
        )

    def share(slot, x, y, block, mine):
        strips = block.reshape(n_sum, strip, width)
        part[slot] = strips.astype(PARTIAL)
        for d in range(1 if mine else 0, n_sum):
            strip_copy(slot, x, y, d).start()
        if mine:
            own[y] = strips

    def pair(slot, x, y, mine):
        left = matched(held[x], ids[x], ids[y])
        right = wide(held.at[y])
        share(slot + 1, y, x, outer(right, left), False)
        share(slot, x, y, outer(left, right), mine)

    def arrive(src):
        for piece in (SLOTS, *range(SLOTS)):
            block_copy(src, piece).wait_recv()

    share(0, me, me, outer(wide(held.at[me]), wide(held.at[me])), True)

    @pl.when(middle)
    def _():
        for piece in (SLOTS, *range(SLOTS)):
            block_copy(near, piece).wait_recv()
            block_copy(near, piece).start()
        pair(1, me, near, True)

        @pl.when(heavy)
        def _():
            arrive(twin)
            pair(3, me, twin, True)

        arrive(far)
        pair(5, me, far, True)

        @pl.when(heavy)
        def _():
            pair(7, near, far, False)

    for y in range(n_tile):
        by_me = jnp.where(middle, jnp.logical_or(y != twin, heavy), y == me)

        def gather(group):
            return pltpu.make_async_remote_copy(
                src_ref=part.at[0, 0],
                dst_ref=landed.at[y, group],
                send_sem=part_send.at[0, 0],
                recv_sem=part_recv.at[y, group],
                device_id=place(twin, group),
                device_id_type=MESH,
            )

        total = None
        for d in range(1, n_sum):
            group = lax.rem(here + d, n_sum)
            gather(group).wait_recv()
            term = landed[y, group].astype(jnp.float32)
            total = term if total is None else total + term

        @pl.when(by_me)
        def _():
            out_ref[:, y * rows : (y + 1) * rows] = total + own[y, here]

        @pl.when(jnp.logical_not(by_me))
        def _():
            gather(here).wait_recv()
            out_ref[:, y * rows : (y + 1) * rows] = total + landed[y, here].astype(jnp.float32)

    def drain_strips(slot, x, mine):
        for d in range(1 if mine else 0, n_sum):
            strip_copy(slot, x, x, d).wait_send()

    @pl.when(jnp.logical_not(heavy))
    def _():
        for piece in range(SLOTS + 1):
            block_copy(me, piece).wait_send()

    drain_strips(0, me, True)

    @pl.when(middle)
    def _():
        for piece in range(SLOTS + 1):
            block_copy(near, piece).wait_send()
        drain_strips(1, me, True)
        drain_strips(2, near, False)
        drain_strips(5, me, True)
        drain_strips(6, far, False)

    @pl.when(heavy)
    def _():
        drain_strips(3, me, True)
        drain_strips(4, twin, False)
        drain_strips(7, near, False)
        drain_strips(8, far, False)


def line_kernel(n_tile, n_cone, n_rep, pattern_hbm, scale_hbm, values_hbm, point_hbm, out_ref,
           pattern_ref, scale_ref, values_ref, point_ref, load_sem, unit_ref, held, ids, part, landed, send_sem, recv_sem, part_send, part_recv):
    rows = values_ref.shape[0]
    cones, width = point_ref.shape
    n_sum = n_cone * n_rep
    strip = rows // n_sum
    me = lax.axis_index("tile")
    here = lax.axis_index("cone") * n_rep + lax.axis_index("rep")
    has_left, has_right = me > 0, me < n_tile - 1

    def peer(d):
        other = lax.rem(here + d, n_sum)
        return other, {"cone": other // n_rep, "rep": lax.rem(other, n_rep)}

    barrier = pltpu.get_barrier_semaphore()

    @pl.when(has_left)
    def _():
        pl.semaphore_signal(barrier, inc=1, device_id={"tile": me - 1}, device_id_type=MESH)

    @pl.when(has_right)
    def _():
        pl.semaphore_signal(barrier, inc=1, device_id={"tile": me + 1}, device_id_type=MESH)

    for d in range(1, n_sum):
        pl.semaphore_signal(barrier, inc=1, device_id=peer(d)[1], device_id_type=MESH)

    waits = load_all(
        (
            (pattern_hbm, pattern_ref),
            (scale_hbm, scale_ref),
            (point_hbm, point_ref),
            (values_hbm, values_ref),
        ),
        load_sem,
    )

    def block_copy(src, piece, right):
        ref = ids.at[src] if piece == SLOTS else held.at[src, piece]
        return pltpu.make_async_remote_copy(
            src_ref=ref,
            dst_ref=ref,
            send_sem=send_sem.at[0 if right else 1, src, piece],
            recv_sem=recv_sem.at[src, piece],
            device_id={"tile": me + 1 if right else me - 1},
            device_id_type=MESH,
        )

    def send_own(piece):
        @pl.when(has_right)
        def _():
            block_copy(me, piece, True).start()

        @pl.when(has_left)
        def _():
            block_copy(me, piece, False).start()

    def on_ids():
        pl.semaphore_wait(
            barrier, has_left.astype(jnp.int32) + has_right.astype(jnp.int32) + (n_sum - 1)
        )
        send_own(SLOTS)

    pack(pattern_ref, scale_ref, values_ref, point_ref, unit_ref, ids.at[me], held.at[me], waits, on_ids, send_own)

    def part_copy(src, d):
        other, device = peer(d)
        return pltpu.make_async_remote_copy(
            src_ref=part.at[src, other],
            dst_ref=landed.at[src, d - 1],
            send_sem=part_send.at[src, d - 1],
            recv_sem=part_recv.at[src, d - 1],
            device_id=device,
            device_id_type=MESH,
        )

    def product(src, own):
        left = wide(held.at[me]) if own else matched(held[me], ids[me], ids[src])
        block = outer(left, wide(held.at[src]))
        part[src] = block.reshape(n_sum, strip, width)
        for d in range(1, n_sum):
            part_copy(src, d).start()

    product(me, True)

    def step(s, carry):
        from_left, from_right = me - s, me + s
        for piece in (SLOTS, *range(SLOTS)):
            @pl.when(from_left >= 0)
            def _():
                block_copy(from_left, piece, True).wait_recv()

                @pl.when(has_right)
                def _():
                    block_copy(from_left, piece, True).start()

            @pl.when(from_right < n_tile)
            def _():
                block_copy(from_right, piece, False).wait_recv()

                @pl.when(has_left)
                def _():
                    block_copy(from_right, piece, False).start()

        @pl.when(from_left >= 0)
        def _():
            product(from_left, False)

        @pl.when(from_right < n_tile)
        def _():
            product(from_right, False)

        return carry

    lax.fori_loop(1, n_tile, step, 0)

    for src in range(n_tile):
        total = part[src, here]
        for d in range(1, n_sum):
            part_copy(src, d).wait_recv()
            total = total + landed[src, d - 1]
        out_ref[:, src * rows : (src + 1) * rows] = total

    def drain(src, carry):
        for d in range(1, n_sum):
            part_copy(src, d).wait_send()

        @pl.when(jnp.logical_and(has_right, src <= me))
        def _():
            for piece in range(SLOTS + 1):
                block_copy(src, piece, True).wait_send()

        @pl.when(jnp.logical_and(has_left, src >= me))
        def _():
            for piece in range(SLOTS + 1):
                block_copy(src, piece, False).wait_send()

        return carry

    lax.fori_loop(0, n_tile, drain, 0)


def solution(mesh):
    n_tile, n_cone, n_rep = mesh.shape["tile"], mesh.shape["cone"], mesh.shape["rep"]
    n_sum = n_cone * n_rep

    def per_device(values, pattern, cone_point, cone_scale):
        rows, cols = values.shape
        cones, width = cone_point.shape
        strip = rows // n_sum
        vmem = pl.BlockSpec(memory_space=pltpu.VMEM)
        hbm = pl.BlockSpec(memory_space=pltpu.HBM)
        loads = [
            pltpu.SMEM(pattern.shape, jnp.int32),
            pltpu.SMEM(cone_scale.shape, jnp.float32),
            pltpu.VMEM(values.shape, jnp.bfloat16),
            pltpu.VMEM((cones, width), jnp.float32),
            pltpu.SemaphoreType.DMA((4,)),
            pltpu.VMEM((cones, width), jnp.float32),
            pltpu.VMEM((n_tile, SLOTS, rows, width), jnp.bfloat16),
            pltpu.VMEM((n_tile, 8, width), jnp.int32),
        ]
        if n_tile == 4 and n_rep == 2:
            body = functools.partial(middle_kernel, n_cone, n_rep)
            scratch = [
                pltpu.VMEM((n_tile, n_sum, strip, rows), jnp.float32),
                pltpu.VMEM((9, n_sum, strip, rows), PARTIAL),
                pltpu.VMEM((n_tile, n_sum, strip, rows), PARTIAL),
                pltpu.SemaphoreType.DMA((n_tile, SLOTS + 1)),
                pltpu.SemaphoreType.DMA((n_tile, SLOTS + 1)),
                pltpu.SemaphoreType.DMA((9, n_sum)),
                pltpu.SemaphoreType.DMA((n_tile, n_sum)),
            ]
        else:
            body = functools.partial(line_kernel, n_tile, n_cone, n_rep)
            scratch = [
                pltpu.VMEM((n_tile, n_sum, strip, rows), jnp.float32),
                pltpu.VMEM((n_tile, n_sum - 1, strip, rows), jnp.float32),
                pltpu.SemaphoreType.DMA((2, n_tile, SLOTS + 1)),
                pltpu.SemaphoreType.DMA((n_tile, SLOTS + 1)),
                pltpu.SemaphoreType.DMA((n_tile, n_sum - 1)),
                pltpu.SemaphoreType.DMA((n_tile, n_sum - 1)),
            ]
        return pl.pallas_call(
            body,
            out_shape=jax.ShapeDtypeStruct((strip, n_tile * rows), jnp.float32),
            in_specs=[hbm] * 4,
            out_specs=vmem,
            scratch_shapes=loads + scratch,
            compiler_params=pltpu.CompilerParams(
                collective_id=0, has_side_effects=True, vmem_limit_bytes=60 * 1024 * 1024
            ),
        )(pattern, cone_scale, values, cone_point)

    return jax.shard_map(
        per_device,
        mesh=mesh,
        in_specs=(
            P(("groups", "tile"), ("cone", "rep")),
            P(("groups", "tile"), ("cone", "rep")),
            P(("groups", "cone", "rep"), None),
            P(("groups", "cone", "rep")),
        ),
        out_specs=P(("groups", "tile", "cone", "rep"), None),
        check_vma=False,
    )
```

```python
import functools

import jax
import jax.numpy as jnp
from jax import lax
from jax.experimental import pallas as pl
from jax.experimental.pallas import tpu as pltpu
from jax.sharding import PartitionSpec as P

MESH = pl.DeviceIdType.MESH
SLOTS = 6


PARTIAL = jnp.bfloat16


def pack(pattern_ref, scale_ref, values_ref, point_ref, unit_ref, ids_me, held_me, waits, on_ids, on_slot):
    cones, width = point_ref.shape
    waits[0]()
    chosen = [[] for _ in range(SLOTS)]
    count = jnp.int32(0)
    for k in range(cones):
        live = pattern_ref[0, k]
        for s in range(SLOTS):
            chosen[s].append(live * (count == s).astype(jnp.int32) if k >= s else None)
        count = count + live
    for s in range(SLOTS):
        name = sum(chosen[s][k] * (k + 1) for k in range(s, cones))
        ids_me[s : s + 1, :] = jnp.full((1, width), name, jnp.int32)
    on_ids()
    waits[2]()
    lane = lax.broadcasted_iota(jnp.int32, (1, width), 1)
    signs = jnp.where(lane == 0, 1.0, -1.0).astype(jnp.float32)
    point = point_ref[...]
    det = jnp.sum(point * point * signs, axis=1, keepdims=True)
    unit_ref[...] = point / jnp.sqrt(det)
    waits[1]()
    waits[3]()
    for s in range(SLOTS):
        factor, unit, packed = 0.0, 0.0, None
        for k in range(s, cones):
            weight = chosen[s][k].astype(jnp.float32)
            factor = factor + weight * scale_ref[k]
            unit = unit + weight * unit_ref[k : k + 1, :]
            mask = jnp.full((1, width), weight, jnp.float32).astype(jnp.bfloat16)
            term = values_ref[:, k * width : (k + 1) * width] * mask
            packed = term if packed is None else packed + term
        tile = packed.astype(jnp.float32)
        proj = jnp.sum(tile * unit, axis=1, keepdims=True)
        held_me[s] = (factor * (2.0 * proj * unit - tile * signs)).astype(jnp.bfloat16)
        on_slot(s)


def load_all(pairs, load_sem):
    loads = [
        pltpu.make_async_copy(src, dst, load_sem.at[i]) for i, (src, dst) in enumerate(pairs)
    ]
    for load in loads:
        load.start()
    return [load.wait for load in loads]


def matched(first, first_ids, second_ids):
    moved = []
    for b in range(SLOTS):
        total = None
        for a in range(SLOTS):
            same = (first_ids[a : a + 1, :] == second_ids[b : b + 1, :]).astype(jnp.float32)
            term = first[a] * same.astype(jnp.bfloat16)
            total = term if total is None else total + term
        moved.append(total)
    return jnp.concatenate(moved, axis=1)


def wide(ref):
    return jnp.concatenate([ref[s] for s in range(SLOTS)], axis=1)


def outer(x, y):
    return lax.dot_general(
        x, y, (((1,), (1,)), ((), ())), preferred_element_type=jnp.float32
    )


def middle_kernel(n_cone, n_rep, pattern_hbm, scale_hbm, values_hbm, point_hbm, out_ref,
                  pattern_ref, scale_ref, values_ref, point_ref, load_sem, unit_ref, held, ids,
                  own, part, landed, send_sem, recv_sem, part_send, part_recv):
    n_tile = 4
    rows, width = values_ref.shape[0], point_ref.shape[1]
    n_sum = n_cone * n_rep
    strip = rows // n_sum
    me, rep = lax.axis_index("tile"), lax.axis_index("rep")
    here = lax.axis_index("cone") * n_rep + rep
    middle = jnp.logical_or(me == 1, me == 2)
    end = jnp.logical_not(middle)
    twin = n_tile - 1 - me
    near = jnp.where(me < 2, 0, 3)
    far = 3 - near
    heavy = jnp.logical_and(middle, (me == 1) == (rep == 0))
    light = jnp.logical_and(middle, (me == 1) != (rep == 0))

    def place(tile, group):
        return {"tile": tile, "cone": group // n_rep, "rep": lax.rem(group, n_rep)}

    barrier = pltpu.get_barrier_semaphore()
    everyone = n_tile * n_sum
    for d in range(1, everyone):
        other = lax.rem(me * n_sum + here + d, everyone)
        pl.semaphore_signal(
            barrier, inc=1, device_id=place(other // n_sum, lax.rem(other, n_sum)), device_id_type=MESH
        )
    waits = load_all(
        (
            (pattern_hbm, pattern_ref),
            (scale_hbm, scale_ref),
            (point_hbm, point_ref),
            (values_hbm, values_ref),
        ),
        load_sem,
    )

    def block_copy(src, piece):
        ref = ids.at[src] if piece == SLOTS else held.at[src, piece]
        return pltpu.make_async_remote_copy(
            src_ref=ref,
            dst_ref=ref,
            send_sem=send_sem.at[src, piece],
            recv_sem=recv_sem.at[src, piece],
            device_id={"tile": jnp.where(middle, twin, jnp.where(me == 0, 1, 2))},
            device_id_type=MESH,
        )

    def send_own(piece):
        @pl.when(jnp.logical_not(heavy))
        def _():
            block_copy(me, piece).start()

    def on_ids():
        pl.semaphore_wait(barrier, everyone - 1)
        send_own(SLOTS)

    pack(pattern_ref, scale_ref, values_ref, point_ref, unit_ref, ids.at[me], held.at[me], waits, on_ids, send_own)

    def strip_copy(slot, x, y, d):
        group = lax.rem(here + d, n_sum)
        return pltpu.make_async_remote_copy(
            src_ref=part.at[slot, group],
            dst_ref=landed.at[y, here],
            send_sem=part_send.at[slot, group],
            recv_sem=part_recv.at[y, here],
            device_id=place(x, group),
            device_id_type=MESH,
        )

    def share(slot, x, y, block, mine):
        strips = block.reshape(n_sum, strip, width)
        part[slot] = strips.astype(PARTIAL)
        for d in range(1 if mine else 0, n_sum):
            strip_copy(slot, x, y, d).start()
        if mine:
            own[y] = strips

    def pair(slot, x, y, mine):
        left = matched(held[x], ids[x], ids[y])
        right = wide(held.at[y])
        share(slot + 1, y, x, outer(right, left), False)
        share(slot, x, y, outer(left, right), mine)

    def arrive(src):
        for piece in (SLOTS, *range(SLOTS)):
            block_copy(src, piece).wait_recv()

    share(0, me, me, outer(wide(held.at[me]), wide(held.at[me])), True)

    @pl.when(light)
    def _():
        for piece in (SLOTS, *range(SLOTS)):
            block_copy(near, piece).wait_recv()
            block_copy(near, piece).start()
        pair(1, me, near, True)

    @pl.when(heavy)
    def _():
        arrive(twin)
        pair(3, me, twin, True)
        arrive(near)
        pair(1, me, near, True)
        pair(5, near, twin, False)
        arrive(far)
        pair(7, me, far, True)
        pair(9, near, far, False)

    for y in range(n_tile):
        by_me = jnp.logical_or(heavy, jnp.logical_or(y == me, jnp.logical_and(light, y == near)))

        def gather(group):
            return pltpu.make_async_remote_copy(
                src_ref=part.at[0, 0],
                dst_ref=landed.at[y, group],
                send_sem=part_send.at[0, 0],
                recv_sem=part_recv.at[y, group],
                device_id=place(twin, group),
                device_id_type=MESH,
            )

        total = None
        for d in range(1, n_sum):
            group = lax.rem(here + d, n_sum)
            gather(group).wait_recv()
            term = landed[y, group].astype(jnp.float32)
            total = term if total is None else total + term

        @pl.when(by_me)
        def _():
            out_ref[:, y * rows : (y + 1) * rows] = total + own[y, here]

        @pl.when(jnp.logical_not(by_me))
        def _():
            gather(here).wait_recv()
            out_ref[:, y * rows : (y + 1) * rows] = total + landed[y, here].astype(jnp.float32)

    def drain_strips(slot, x, mine):
        for d in range(1 if mine else 0, n_sum):
            strip_copy(slot, x, x, d).wait_send()

    @pl.when(jnp.logical_not(heavy))
    def _():
        for piece in range(SLOTS + 1):
            block_copy(me, piece).wait_send()

    drain_strips(0, me, True)

    @pl.when(middle)
    def _():
        drain_strips(1, me, True)
        drain_strips(2, near, False)

    @pl.when(light)
    def _():
        for piece in range(SLOTS + 1):
            block_copy(near, piece).wait_send()

    @pl.when(heavy)
    def _():
        drain_strips(3, me, True)
        drain_strips(4, twin, False)
        drain_strips(5, near, False)
        drain_strips(6, twin, False)
        drain_strips(7, me, True)
        drain_strips(8, far, False)
        drain_strips(9, near, False)
        drain_strips(10, far, False)


def line_kernel(n_tile, n_cone, n_rep, pattern_hbm, scale_hbm, values_hbm, point_hbm, out_ref,
           pattern_ref, scale_ref, values_ref, point_ref, load_sem, unit_ref, held, ids, part, landed, send_sem, recv_sem, part_send, part_recv):
    rows = values_ref.shape[0]
    cones, width = point_ref.shape
    n_sum = n_cone * n_rep
    strip = rows // n_sum
    me = lax.axis_index("tile")
    here = lax.axis_index("cone") * n_rep + lax.axis_index("rep")
    has_left, has_right = me > 0, me < n_tile - 1

    def peer(d):
        other = lax.rem(here + d, n_sum)
        return other, {"cone": other // n_rep, "rep": lax.rem(other, n_rep)}

    barrier = pltpu.get_barrier_semaphore()

    @pl.when(has_left)
    def _():
        pl.semaphore_signal(barrier, inc=1, device_id={"tile": me - 1}, device_id_type=MESH)

    @pl.when(has_right)
    def _():
        pl.semaphore_signal(barrier, inc=1, device_id={"tile": me + 1}, device_id_type=MESH)

    for d in range(1, n_sum):
        pl.semaphore_signal(barrier, inc=1, device_id=peer(d)[1], device_id_type=MESH)

    waits = load_all(
        (
            (pattern_hbm, pattern_ref),
            (scale_hbm, scale_ref),
            (point_hbm, point_ref),
            (values_hbm, values_ref),
        ),
        load_sem,
    )

    def block_copy(src, piece, right):
        ref = ids.at[src] if piece == SLOTS else held.at[src, piece]
        return pltpu.make_async_remote_copy(
            src_ref=ref,
            dst_ref=ref,
            send_sem=send_sem.at[0 if right else 1, src, piece],
            recv_sem=recv_sem.at[src, piece],
            device_id={"tile": me + 1 if right else me - 1},
            device_id_type=MESH,
        )

    def send_own(piece):
        @pl.when(has_right)
        def _():
            block_copy(me, piece, True).start()

        @pl.when(has_left)
        def _():
            block_copy(me, piece, False).start()

    def on_ids():
        pl.semaphore_wait(
            barrier, has_left.astype(jnp.int32) + has_right.astype(jnp.int32) + (n_sum - 1)
        )
        send_own(SLOTS)

    pack(pattern_ref, scale_ref, values_ref, point_ref, unit_ref, ids.at[me], held.at[me], waits, on_ids, send_own)

    def part_copy(src, d):
        other, device = peer(d)
        return pltpu.make_async_remote_copy(
            src_ref=part.at[src, other],
            dst_ref=landed.at[src, d - 1],
            send_sem=part_send.at[src, d - 1],
            recv_sem=part_recv.at[src, d - 1],
            device_id=device,
            device_id_type=MESH,
        )

    def product(src, own):
        left = wide(held.at[me]) if own else matched(held[me], ids[me], ids[src])
        block = outer(left, wide(held.at[src]))
        part[src] = block.reshape(n_sum, strip, width)
        for d in range(1, n_sum):
            part_copy(src, d).start()

    product(me, True)

    def step(s, carry):
        from_left, from_right = me - s, me + s
        for piece in (SLOTS, *range(SLOTS)):
            @pl.when(from_left >= 0)
            def _():
                block_copy(from_left, piece, True).wait_recv()

                @pl.when(has_right)
                def _():
                    block_copy(from_left, piece, True).start()

            @pl.when(from_right < n_tile)
            def _():
                block_copy(from_right, piece, False).wait_recv()

                @pl.when(has_left)
                def _():
                    block_copy(from_right, piece, False).start()

        @pl.when(from_left >= 0)
        def _():
            product(from_left, False)

        @pl.when(from_right < n_tile)
        def _():
            product(from_right, False)

        return carry

    lax.fori_loop(1, n_tile, step, 0)

    for src in range(n_tile):
        total = part[src, here]
        for d in range(1, n_sum):
            part_copy(src, d).wait_recv()
            total = total + landed[src, d - 1]
        out_ref[:, src * rows : (src + 1) * rows] = total

    def drain(src, carry):
        for d in range(1, n_sum):
            part_copy(src, d).wait_send()

        @pl.when(jnp.logical_and(has_right, src <= me))
        def _():
            for piece in range(SLOTS + 1):
                block_copy(src, piece, True).wait_send()

        @pl.when(jnp.logical_and(has_left, src >= me))
        def _():
            for piece in range(SLOTS + 1):
                block_copy(src, piece, False).wait_send()

        return carry

    lax.fori_loop(0, n_tile, drain, 0)


def solution(mesh):
    n_tile, n_cone, n_rep = mesh.shape["tile"], mesh.shape["cone"], mesh.shape["rep"]
    n_sum = n_cone * n_rep

    def per_device(values, pattern, cone_point, cone_scale):
        rows, cols = values.shape
        cones, width = cone_point.shape
        strip = rows // n_sum
        vmem = pl.BlockSpec(memory_space=pltpu.VMEM)
        hbm = pl.BlockSpec(memory_space=pltpu.HBM)
        loads = [
            pltpu.SMEM(pattern.shape, jnp.int32),
            pltpu.SMEM(cone_scale.shape, jnp.float32),
            pltpu.VMEM(values.shape, jnp.bfloat16),
            pltpu.VMEM((cones, width), jnp.float32),
            pltpu.SemaphoreType.DMA((4,)),
            pltpu.VMEM((cones, width), jnp.float32),
            pltpu.VMEM((n_tile, SLOTS, rows, width), jnp.bfloat16),
            pltpu.VMEM((n_tile, 8, width), jnp.int32),
        ]
        if n_tile == 4 and n_rep == 2:
            body = functools.partial(middle_kernel, n_cone, n_rep)
            scratch = [
                pltpu.VMEM((n_tile, n_sum, strip, rows), jnp.float32),
                pltpu.VMEM((11, n_sum, strip, rows), PARTIAL),
                pltpu.VMEM((n_tile, n_sum, strip, rows), PARTIAL),
                pltpu.SemaphoreType.DMA((n_tile, SLOTS + 1)),
                pltpu.SemaphoreType.DMA((n_tile, SLOTS + 1)),
                pltpu.SemaphoreType.DMA((11, n_sum)),
                pltpu.SemaphoreType.DMA((n_tile, n_sum)),
            ]
        else:
            body = functools.partial(line_kernel, n_tile, n_cone, n_rep)
            scratch = [
                pltpu.VMEM((n_tile, n_sum, strip, rows), jnp.float32),
                pltpu.VMEM((n_tile, n_sum - 1, strip, rows), jnp.float32),
                pltpu.SemaphoreType.DMA((2, n_tile, SLOTS + 1)),
                pltpu.SemaphoreType.DMA((n_tile, SLOTS + 1)),
                pltpu.SemaphoreType.DMA((n_tile, n_sum - 1)),
                pltpu.SemaphoreType.DMA((n_tile, n_sum - 1)),
            ]
        return pl.pallas_call(
            body,
            out_shape=pltpu.VMEM((strip, n_tile * rows), jnp.float32),
            in_specs=[hbm] * 4,
            out_specs=vmem,
            scratch_shapes=loads + scratch,
            compiler_params=pltpu.CompilerParams(
                collective_id=0, has_side_effects=True, vmem_limit_bytes=60 * 1024 * 1024
            ),
        )(pattern, cone_scale, values, cone_point)

    return jax.shard_map(
        per_device,
        mesh=mesh,
        in_specs=(
            P(("groups", "tile"), ("cone", "rep")),
            P(("groups", "tile"), ("cone", "rep")),
            P(("groups", "cone", "rep"), None),
            P(("groups", "cone", "rep")),
        ),
        out_specs=P(("groups", "tile", "cone", "rep"), None),
        check_vma=False,
    )
```

```python
import functools

import jax
import jax.numpy as jnp
from jax import lax
from jax.experimental import pallas as pl
from jax.experimental.pallas import tpu as pltpu
from jax.sharding import PartitionSpec as P

MESH = pl.DeviceIdType.MESH
SLOTS = 6


PARTIAL = jnp.bfloat16


def pack(pattern_ref, scale_ref, values_ref, point_ref, unit_ref, ids_me, held_me, waits, on_ids, on_strip):
    cones, width = point_ref.shape
    waits[0]()
    chosen = [[] for _ in range(SLOTS)]
    count = jnp.int32(0)
    for k in range(cones):
        live = pattern_ref[0, k]
        for s in range(SLOTS):
            chosen[s].append(live * (count == s).astype(jnp.int32) if k >= s else None)
        count = count + live
    for s in range(SLOTS):
        name = sum(chosen[s][k] * (k + 1) for k in range(s, cones))
        ids_me[s : s + 1, :] = jnp.full((1, width), name, jnp.int32)
    on_ids()
    waits[2]()
    lane = lax.broadcasted_iota(jnp.int32, (1, width), 1)
    signs = jnp.where(lane == 0, 1.0, -1.0).astype(jnp.float32)
    point = point_ref[...]
    det = jnp.sum(point * point * signs, axis=1, keepdims=True)
    unit_ref[...] = point / jnp.sqrt(det)
    waits[1]()
    waits[3]()
    slots = []
    for s in range(SLOTS):
        factor, unit, masks = 0.0, 0.0, []
        for k in range(s, cones):
            weight = chosen[s][k].astype(jnp.float32)
            factor = factor + weight * scale_ref[k]
            unit = unit + weight * unit_ref[k : k + 1, :]
            masks.append(jnp.full((1, width), weight, jnp.float32).astype(jnp.bfloat16))
        slots.append((factor, unit, masks))
    strip = held_me.shape[2]
    for q in range(held_me.shape[0]):
        for s, (factor, unit, masks) in enumerate(slots):
            packed = None
            for k, mask in zip(range(s, cones), masks):
                term = values_ref[q * strip : (q + 1) * strip, k * width : (k + 1) * width] * mask
                packed = term if packed is None else packed + term
            tile = packed.astype(jnp.float32)
            proj = jnp.sum(tile * unit, axis=1, keepdims=True)
            held_me[q, s] = (factor * (2.0 * proj * unit - tile * signs)).astype(jnp.bfloat16)
        on_strip(q)


def load_all(pairs, load_sem):
    loads = [
        pltpu.make_async_copy(src, dst, load_sem.at[i]) for i, (src, dst) in enumerate(pairs)
    ]
    for load in loads:
        load.start()
    return [load.wait for load in loads]


def slots_of(ref):
    return [ref[:, s].reshape(-1, ref.shape[3]) for s in range(SLOTS)]


def wide(ref):
    return jnp.concatenate(slots_of(ref), axis=1)


def matched(first, first_ids, second_ids):
    moved = []
    tiles = slots_of(first)
    for b in range(SLOTS):
        total = None
        for a in range(SLOTS):
            same = (first_ids[a : a + 1, :] == second_ids[b : b + 1, :]).astype(jnp.float32)
            term = tiles[a] * same.astype(jnp.bfloat16)
            total = term if total is None else total + term
        moved.append(total)
    return jnp.concatenate(moved, axis=1)


def outer(x, y):
    return lax.dot_general(
        x, y, (((1,), (1,)), ((), ())), preferred_element_type=jnp.float32
    )


def middle_kernel(n_cone, n_rep, pattern_hbm, scale_hbm, values_hbm, point_hbm, out_ref,
                  pattern_ref, scale_ref, values_ref, point_ref, load_sem, unit_ref, held, ids,
                  own, part, landed, send_sem, recv_sem, part_send, part_recv):
    n_tile = 4
    rows, width = values_ref.shape[0], point_ref.shape[1]
    n_sum = n_cone * n_rep
    strip = rows // n_sum
    me, rep = lax.axis_index("tile"), lax.axis_index("rep")
    here = lax.axis_index("cone") * n_rep + rep
    heavy_tile = 1 + rep
    heavy = me == heavy_tile
    twin = 3 - heavy_tile
    near = 3 * rep
    far = 3 - near

    waits = load_all(
        (
            (pattern_hbm, pattern_ref),
            (scale_hbm, scale_ref),
            (point_hbm, point_ref),
            (values_hbm, values_ref),
        ),
        load_sem,
    )

    def place(tile, group):
        return {"tile": tile, "cone": group // n_rep, "rep": lax.rem(group, n_rep)}

    barrier = pltpu.get_barrier_semaphore()
    everyone = n_tile * n_sum
    for d in range(1, everyone):
        other = lax.rem(me * n_sum + here + d, everyone)
        pl.semaphore_signal(
            barrier, inc=1, device_id=place(other // n_sum, lax.rem(other, n_sum)), device_id_type=MESH
        )

    def block_copy(src, piece):
        ref = ids.at[src] if piece == n_sum else held.at[src, piece]
        return pltpu.make_async_remote_copy(
            src_ref=ref,
            dst_ref=ref,
            send_sem=send_sem.at[src, piece],
            recv_sem=recv_sem.at[src, piece],
            device_id={"tile": heavy_tile},
            device_id_type=MESH,
        )

    def send_own(piece):
        @pl.when(jnp.logical_not(heavy))
        def _():
            block_copy(me, piece).start()

    def on_ids():
        pl.semaphore_wait(barrier, everyone - 1)
        send_own(n_sum)

    pack(pattern_ref, scale_ref, values_ref, point_ref, unit_ref, ids.at[me], held.at[me], waits, on_ids, send_own)

    def strip_copy(slot, x, y, group, count=1):
        return pltpu.make_async_remote_copy(
            src_ref=part.at[pl.ds(slot, count), group],
            dst_ref=landed.at[pl.ds(y, count), here],
            send_sem=part_send.at[slot, group],
            recv_sem=part_recv.at[y, here],
            device_id=place(x, group),
            device_id_type=MESH,
        )

    def send(slot, x, y, mine, count=1):
        for d in range(1 if mine else 0, n_sum):
            strip_copy(slot, x, y, lax.rem(here + d, n_sum), count).start()

    def drain(slot, x, y, mine, count=1):
        for d in range(1 if mine else 0, n_sum):
            strip_copy(slot, x, y, lax.rem(here + d, n_sum), count).wait_send()

    def put(slot, block, y=None):
        strips = block.reshape(n_sum, strip, width)
        part[slot] = strips.astype(PARTIAL)
        if y is not None:
            own[y] = strips

    def arrive(src, piece):
        block_copy(src, piece).wait_recv()

    def moved(blocks, to):
        return jnp.concatenate([matched(held.at[x], ids[x], ids[to]) for x in blocks], axis=0)

    low = heavy_tile - 1
    diagonal_send = (0, me, me, True, 1)
    twin_sends = ((0, me, 1, True, 2), (2, twin, me, False, 1))
    near_send = (4, near, 1, False, 2)
    near_sends = ((3, twin, near, False, 1), (7, me, near, True, 1))
    far_send = (9, far, low, False, 3)
    far_sends = ((6, near, far, False, 1), (12, twin, far, False, 1), (8, me, far, True, 1))

    put(jnp.where(heavy, low, 0), outer(wide(held.at[me]), wide(held.at[me])), me)

    @pl.when(jnp.logical_not(heavy))
    def _():
        send(*diagonal_send)

    @pl.when(heavy)
    def _():
        for piece in (n_sum, *range(n_sum)):
            arrive(twin, piece)
        left, right = moved((me,), twin), wide(held.at[twin])
        put(2, outer(right, left))
        put(twin - 1, outer(left, right), twin)
        for message in twin_sends:
            send(*message)

        arrive(near, n_sum)
        left = moved((me, twin), near)
        for q in range(n_sum):
            arrive(near, q)
        right = wide(held.at[near])
        block = outer(right, left)
        put(4 + me - 1, block[:, :width])
        put(4 + twin - 1, block[:, width:])
        send(*near_send)
        block = outer(left, right)
        put(7, block[:rows], near)
        put(3, block[rows:])
        for message in near_sends:
            send(*message)

        arrive(far, n_sum)
        left = moved((me, near, twin), far)
        for q in range(n_sum):
            arrive(far, q)
        right = wide(held.at[far])
        block = outer(right, left)
        put(9 + me - low, block[:, :width])
        put(9 + near - low, block[:, width : 2 * width])
        put(9 + twin - low, block[:, 2 * width :])
        send(*far_send)
        block = outer(left, right)
        put(8, block[:rows], far)
        put(6, block[rows : 2 * rows])
        put(12, block[2 * rows :])
        for message in far_sends:
            send(*message)

    def expect(y, group, count=1):
        pltpu.make_async_remote_copy(
            src_ref=part.at[pl.ds(0, count), 0],
            dst_ref=landed.at[pl.ds(y, count), group],
            send_sem=part_send.at[0, 0],
            recv_sem=part_recv.at[y, group],
            device_id=place(lax.rem(me + 1, n_tile), group),
            device_id_type=MESH,
        ).wait_recv()

    for group in range(n_sum):
        h, n = 1 + group % n_rep, 3 * (group % n_rep)
        l, f = 3 - h, 3 - n

        @pl.when(jnp.logical_and(me == h, here != group))
        def _():
            expect(1, group, 2)
            expect(n, group)
            expect(f, group)

        @pl.when(me == l)
        def _():
            expect(h, group)
            expect(n, group)
            expect(f, group)

        @pl.when(me == n)
        def _():
            expect(1, group, 2)
            expect(f, group)

        @pl.when(me == f)
        def _():
            expect(h - 1, group, 3)

        @pl.when(jnp.logical_and(me != h, here != group))
        def _():
            expect(me, group)

    for y in range(n_tile):
        by_me = jnp.logical_or(heavy, y == me)
        total = None
        for d in range(1, n_sum):
            term = landed[y, lax.rem(here + d, n_sum)].astype(jnp.float32)
            total = term if total is None else total + term

        @pl.when(by_me)
        def _():
            out_ref[:, y * rows : (y + 1) * rows] = total + own[y, here]

        @pl.when(jnp.logical_not(by_me))
        def _():
            out_ref[:, y * rows : (y + 1) * rows] = total + landed[y, here].astype(jnp.float32)

    @pl.when(jnp.logical_not(heavy))
    def _():
        for piece in range(n_sum + 1):
            block_copy(me, piece).wait_send()
        drain(*diagonal_send)

    @pl.when(heavy)
    def _():
        for message in (*twin_sends, near_send, *near_sends, far_send, *far_sends):
            drain(*message)


def line_kernel(n_tile, n_cone, n_rep, pattern_hbm, scale_hbm, values_hbm, point_hbm, out_ref,
           pattern_ref, scale_ref, values_ref, point_ref, load_sem, unit_ref, held, ids, part, landed, send_sem, recv_sem, part_send, part_recv):
    rows = values_ref.shape[0]
    cones, width = point_ref.shape
    n_sum = n_cone * n_rep
    strip = rows // n_sum
    me = lax.axis_index("tile")
    here = lax.axis_index("cone") * n_rep + lax.axis_index("rep")
    has_left, has_right = me > 0, me < n_tile - 1

    def peer(d):
        other = lax.rem(here + d, n_sum)
        return other, {"cone": other // n_rep, "rep": lax.rem(other, n_rep)}

    barrier = pltpu.get_barrier_semaphore()

    @pl.when(has_left)
    def _():
        pl.semaphore_signal(barrier, inc=1, device_id={"tile": me - 1}, device_id_type=MESH)

    @pl.when(has_right)
    def _():
        pl.semaphore_signal(barrier, inc=1, device_id={"tile": me + 1}, device_id_type=MESH)

    for d in range(1, n_sum):
        pl.semaphore_signal(barrier, inc=1, device_id=peer(d)[1], device_id_type=MESH)

    waits = load_all(
        (
            (pattern_hbm, pattern_ref),
            (scale_hbm, scale_ref),
            (point_hbm, point_ref),
            (values_hbm, values_ref),
        ),
        load_sem,
    )

    def block_copy(src, piece, right):
        ref = ids.at[src] if piece == n_sum else held.at[src, piece]
        return pltpu.make_async_remote_copy(
            src_ref=ref,
            dst_ref=ref,
            send_sem=send_sem.at[0 if right else 1, src, piece],
            recv_sem=recv_sem.at[src, piece],
            device_id={"tile": me + 1 if right else me - 1},
            device_id_type=MESH,
        )

    def send_own(piece):
        @pl.when(has_right)
        def _():
            block_copy(me, piece, True).start()

        @pl.when(has_left)
        def _():
            block_copy(me, piece, False).start()

    def on_ids():
        pl.semaphore_wait(
            barrier, has_left.astype(jnp.int32) + has_right.astype(jnp.int32) + (n_sum - 1)
        )
        send_own(n_sum)

    pack(pattern_ref, scale_ref, values_ref, point_ref, unit_ref, ids.at[me], held.at[me], waits, on_ids, send_own)

    def part_copy(src, d):
        other, device = peer(d)
        return pltpu.make_async_remote_copy(
            src_ref=part.at[src, other],
            dst_ref=landed.at[src, d - 1],
            send_sem=part_send.at[src, d - 1],
            recv_sem=part_recv.at[src, d - 1],
            device_id=device,
            device_id_type=MESH,
        )

    def product(src, own):
        left = wide(held.at[me]) if own else matched(held.at[me], ids[me], ids[src])
        block = outer(left, wide(held.at[src]))
        part[src] = block.reshape(n_sum, strip, width)
        for d in range(1, n_sum):
            part_copy(src, d).start()

    product(me, True)

    def step(s, carry):
        from_left, from_right = me - s, me + s
        for piece in (n_sum, *range(n_sum)):
            @pl.when(from_left >= 0)
            def _():
                block_copy(from_left, piece, True).wait_recv()

                @pl.when(has_right)
                def _():
                    block_copy(from_left, piece, True).start()

            @pl.when(from_right < n_tile)
            def _():
                block_copy(from_right, piece, False).wait_recv()

                @pl.when(has_left)
                def _():
                    block_copy(from_right, piece, False).start()

        @pl.when(from_left >= 0)
        def _():
            product(from_left, False)

        @pl.when(from_right < n_tile)
        def _():
            product(from_right, False)

        return carry

    lax.fori_loop(1, n_tile, step, 0)

    for src in range(n_tile):
        total = part[src, here]
        for d in range(1, n_sum):
            part_copy(src, d).wait_recv()
            total = total + landed[src, d - 1]
        out_ref[:, src * rows : (src + 1) * rows] = total

    def drain(src, carry):
        for d in range(1, n_sum):
            part_copy(src, d).wait_send()

        @pl.when(jnp.logical_and(has_right, src <= me))
        def _():
            for piece in range(n_sum + 1):
                block_copy(src, piece, True).wait_send()

        @pl.when(jnp.logical_and(has_left, src >= me))
        def _():
            for piece in range(n_sum + 1):
                block_copy(src, piece, False).wait_send()

        return carry

    lax.fori_loop(0, n_tile, drain, 0)


def solution(mesh):
    n_tile, n_cone, n_rep = mesh.shape["tile"], mesh.shape["cone"], mesh.shape["rep"]
    n_sum = n_cone * n_rep

    def per_device(values, pattern, cone_point, cone_scale):
        rows, cols = values.shape
        cones, width = cone_point.shape
        strip = rows // n_sum
        vmem = pl.BlockSpec(memory_space=pltpu.VMEM)
        hbm = pl.BlockSpec(memory_space=pltpu.HBM)
        loads = [
            pltpu.SMEM(pattern.shape, jnp.int32),
            pltpu.SMEM(cone_scale.shape, jnp.float32),
            pltpu.VMEM(values.shape, jnp.bfloat16),
            pltpu.VMEM((cones, width), jnp.float32),
            pltpu.SemaphoreType.DMA((4,)),
            pltpu.VMEM((cones, width), jnp.float32),
            pltpu.VMEM((n_tile, n_sum, SLOTS, strip, width), jnp.bfloat16),
            pltpu.VMEM((n_tile, 8, width), jnp.int32),
        ]
        if n_tile == 4 and n_rep == 2:
            body = functools.partial(middle_kernel, n_cone, n_rep)
            scratch = [
                pltpu.VMEM((n_tile, n_sum, strip, rows), jnp.float32),
                pltpu.VMEM((13, n_sum, strip, rows), PARTIAL),
                pltpu.VMEM((n_tile, n_sum, strip, rows), PARTIAL),
                pltpu.SemaphoreType.DMA((n_tile, n_sum + 1)),
                pltpu.SemaphoreType.DMA((n_tile, n_sum + 1)),
                pltpu.SemaphoreType.DMA((13, n_sum)),
                pltpu.SemaphoreType.DMA((n_tile, n_sum)),
            ]
        else:
            body = functools.partial(line_kernel, n_tile, n_cone, n_rep)
            scratch = [
                pltpu.VMEM((n_tile, n_sum, strip, rows), jnp.float32),
                pltpu.VMEM((n_tile, n_sum - 1, strip, rows), jnp.float32),
                pltpu.SemaphoreType.DMA((2, n_tile, n_sum + 1)),
                pltpu.SemaphoreType.DMA((n_tile, n_sum + 1)),
                pltpu.SemaphoreType.DMA((n_tile, n_sum - 1)),
                pltpu.SemaphoreType.DMA((n_tile, n_sum - 1)),
            ]
        return pl.pallas_call(
            body,
            out_shape=pltpu.VMEM((strip, n_tile * rows), jnp.float32),
            in_specs=[hbm] * 4,
            out_specs=vmem,
            scratch_shapes=loads + scratch,
            compiler_params=pltpu.CompilerParams(
                collective_id=0, has_side_effects=True, vmem_limit_bytes=60 * 1024 * 1024
            ),
        )(pattern, cone_scale, values, cone_point)

    return jax.shard_map(
        per_device,
        mesh=mesh,
        in_specs=(
            P(("groups", "tile"), ("cone", "rep")),
            P(("groups", "tile"), ("cone", "rep")),
            P(("groups", "cone", "rep"), None),
            P(("groups", "cone", "rep")),
        ),
        out_specs=P(("groups", "tile", "cone", "rep"), None),
        check_vma=False,
    )
```

```python
import functools

import jax
import jax.numpy as jnp
from jax import lax
from jax.experimental import pallas as pl
from jax.experimental.pallas import tpu as pltpu
from jax.sharding import PartitionSpec as P

MESH = pl.DeviceIdType.MESH
SLOTS = 6


PARTIAL = jnp.bfloat16


def pack(pattern_ref, scale_ref, values_ref, point_ref, unit_ref, ids_me, held_me, waits, on_ids, on_strip):
    cones, width = point_ref.shape
    waits[0]()
    chosen = [[] for _ in range(SLOTS)]
    count = jnp.int32(0)
    for k in range(cones):
        live = pattern_ref[0, k]
        for s in range(SLOTS):
            chosen[s].append(live * (count == s).astype(jnp.int32) if k >= s else None)
        count = count + live
    for s in range(SLOTS):
        name = sum(chosen[s][k] * (k + 1) for k in range(s, cones))
        ids_me[s : s + 1, :] = jnp.full((1, width), name, jnp.int32)
    on_ids()
    waits[2]()
    lane = lax.broadcasted_iota(jnp.int32, (1, width), 1)
    signs = jnp.where(lane == 0, 1.0, -1.0).astype(jnp.float32)
    point = point_ref[...]
    det = jnp.sum(point * point * signs, axis=1, keepdims=True)
    unit_ref[...] = point / jnp.sqrt(det)
    waits[1]()
    slots = []
    for s in range(SLOTS):
        factor, unit, masks = 0.0, 0.0, []
        for k in range(s, cones):
            weight = chosen[s][k].astype(jnp.float32)
            factor = factor + weight * scale_ref[k]
            unit = unit + weight * unit_ref[k : k + 1, :]
            masks.append(jnp.full((1, width), weight, jnp.float32).astype(jnp.bfloat16))
        slots.append((factor, unit, masks))
    strip = held_me.shape[2]
    for q in range(held_me.shape[0]):
        waits[3 + q]()
        for s, (factor, unit, masks) in enumerate(slots):
            packed = None
            for k, mask in zip(range(s, cones), masks):
                term = values_ref[q * strip : (q + 1) * strip, k * width : (k + 1) * width] * mask
                packed = term if packed is None else packed + term
            tile = packed.astype(jnp.float32)
            proj = jnp.sum(tile * unit, axis=1, keepdims=True)
            held_me[q, s] = (factor * (2.0 * proj * unit - tile * signs)).astype(jnp.bfloat16)
        on_strip(q)


def load_all(pairs, load_sem):
    loads = [
        pltpu.make_async_copy(src, dst, load_sem.at[i]) for i, (src, dst) in enumerate(pairs)
    ]
    for load in loads:
        load.start()
    return [load.wait for load in loads]


def slots_of(ref):
    return [ref[:, s].reshape(-1, ref.shape[3]) for s in range(SLOTS)]


def wide(ref):
    return jnp.concatenate(slots_of(ref), axis=1)


def matched(first, first_ids, second_ids):
    moved = []
    tiles = slots_of(first)
    for b in range(SLOTS):
        total = None
        for a in range(SLOTS):
            same = (first_ids[a : a + 1, :] == second_ids[b : b + 1, :]).astype(jnp.float32)
            term = tiles[a] * same.astype(jnp.bfloat16)
            total = term if total is None else total + term
        moved.append(total)
    return jnp.concatenate(moved, axis=1)


def outer(x, y):
    return lax.dot_general(
        x, y, (((1,), (1,)), ((), ())), preferred_element_type=jnp.float32
    )


def middle_kernel(n_cone, n_rep, pattern_hbm, scale_hbm, values_hbm, point_hbm, out_ref,
                  pattern_ref, scale_ref, values_ref, point_ref, load_sem, unit_ref, held, ids,
                  own, part, landed, send_sem, recv_sem, part_send, part_recv, turn):
    n_tile = 4
    rows, width = values_ref.shape[0], point_ref.shape[1]
    n_sum = n_cone * n_rep
    strip = rows // n_sum
    me, rep = lax.axis_index("tile"), lax.axis_index("rep")
    here = lax.axis_index("cone") * n_rep + rep
    heavy_tile = 1 + rep
    heavy = me == heavy_tile
    twin = 3 - heavy_tile
    near = 3 * rep
    far = 3 - near

    waits = load_all(
        (
            (pattern_hbm, pattern_ref),
            (scale_hbm, scale_ref),
            (point_hbm, point_ref),
            *(
                (values_hbm.at[pl.ds(q * strip, strip)], values_ref.at[pl.ds(q * strip, strip)])
                for q in range(n_sum)
            ),
        ),
        load_sem,
    )

    def place(tile, group):
        return {"tile": tile, "cone": group // n_rep, "rep": lax.rem(group, n_rep)}

    barrier = pltpu.get_barrier_semaphore()
    everyone = n_tile * n_sum
    for d in range(1, everyone):
        other = lax.rem(me * n_sum + here + d, everyone)
        pl.semaphore_signal(
            barrier, inc=1, device_id=place(other // n_sum, lax.rem(other, n_sum)), device_id_type=MESH
        )

    def block_copy(src, piece):
        ref = ids.at[src] if piece == n_sum else held.at[src, piece]
        return pltpu.make_async_remote_copy(
            src_ref=ref,
            dst_ref=ref,
            send_sem=send_sem.at[src, piece],
            recv_sem=recv_sem.at[src, piece],
            device_id={"tile": heavy_tile},
            device_id_type=MESH,
        )

    def send_own(piece):
        @pl.when(jnp.logical_not(heavy) if piece == n_sum else jnp.logical_or(me == near, me == twin))
        def _():
            block_copy(me, piece).start()

    def on_ids():
        pl.semaphore_wait(barrier, everyone - 1)
        send_own(n_sum)

    pack(pattern_ref, scale_ref, values_ref, point_ref, unit_ref, ids.at[me], held.at[me], waits, on_ids, send_own)

    @pl.when(me == near)
    def _():
        block_copy(me, n_sum // 2).wait_send()
        pl.semaphore_signal(turn, inc=1, device_id={"rep": 1 - rep}, device_id_type=MESH)

    @pl.when(me == far)
    def _():
        pl.semaphore_wait(turn, 1)
        for piece in range(n_sum):
            block_copy(me, piece).start()

    def strip_copy(slot, x, y, group, count=1):
        return pltpu.make_async_remote_copy(
            src_ref=part.at[pl.ds(slot, count), group],
            dst_ref=landed.at[pl.ds(y, count), here],
            send_sem=part_send.at[slot, group],
            recv_sem=part_recv.at[y, here],
            device_id=place(x, group),
            device_id_type=MESH,
        )

    def send(slot, x, y, mine, count=1):
        for d in range(1 if mine else 0, n_sum):
            strip_copy(slot, x, y, lax.rem(here + d, n_sum), count).start()

    def drain(slot, x, y, mine, count=1):
        for d in range(1 if mine else 0, n_sum):
            strip_copy(slot, x, y, lax.rem(here + d, n_sum), count).wait_send()

    def put(slot, block, y=None):
        strips = block.reshape(n_sum, strip, width)
        part[slot] = strips.astype(PARTIAL)
        if y is not None:
            own[y] = strips

    def arrive(src, piece):
        block_copy(src, piece).wait_recv()

    def moved(blocks, to):
        return jnp.concatenate([matched(held.at[x], ids[x], ids[to]) for x in blocks], axis=0)

    low = heavy_tile - 1
    diagonal_send = (0, me, me, True, 1)
    twin_sends = ((0, me, 1, True, 2), (2, twin, me, False, 1))
    near_send = (4, near, 1, False, 2)
    near_sends = ((3, twin, near, False, 1), (7, me, near, True, 1))
    far_send = (9, far, low, False, 3)
    far_sends = ((6, near, far, False, 1), (12, twin, far, False, 1), (8, me, far, True, 1))

    put(jnp.where(heavy, low, 0), outer(wide(held.at[me]), wide(held.at[me])), me)

    @pl.when(jnp.logical_not(heavy))
    def _():
        send(*diagonal_send)

    @pl.when(heavy)
    def _():
        for piece in (n_sum, *range(n_sum)):
            arrive(twin, piece)
        left, right = moved((me,), twin), wide(held.at[twin])
        put(2, outer(right, left))
        put(twin - 1, outer(left, right), twin)
        for message in twin_sends:
            send(*message)

        arrive(near, n_sum)
        left = moved((me, twin), near)
        for q in range(n_sum):
            arrive(near, q)
        right = wide(held.at[near])
        block = outer(right, left)
        put(4 + me - 1, block[:, :width])
        put(4 + twin - 1, block[:, width:])
        send(*near_send)
        block = outer(left, right)
        put(7, block[:rows], near)
        put(3, block[rows:])
        for message in near_sends:
            send(*message)

        arrive(far, n_sum)
        left = moved((me, near, twin), far)
        for q in range(n_sum):
            arrive(far, q)
        right = wide(held.at[far])
        block = outer(right, left)
        put(9 + me - low, block[:, :width])
        put(9 + near - low, block[:, width : 2 * width])
        put(9 + twin - low, block[:, 2 * width :])
        send(*far_send)
        block = outer(left, right)
        put(8, block[:rows], far)
        put(6, block[rows : 2 * rows])
        put(12, block[2 * rows :])
        for message in far_sends:
            send(*message)

    def expect(y, group, count=1):
        pltpu.make_async_remote_copy(
            src_ref=part.at[pl.ds(0, count), 0],
            dst_ref=landed.at[pl.ds(y, count), group],
            send_sem=part_send.at[0, 0],
            recv_sem=part_recv.at[y, group],
            device_id=place(lax.rem(me + 1, n_tile), group),
            device_id_type=MESH,
        ).wait_recv()

    for group in range(n_sum):
        h, n = 1 + group % n_rep, 3 * (group % n_rep)
        l, f = 3 - h, 3 - n

        @pl.when(jnp.logical_and(me == h, here != group))
        def _():
            expect(1, group, 2)
            expect(n, group)
            expect(f, group)

        @pl.when(me == l)
        def _():
            expect(h, group)
            expect(n, group)
            expect(f, group)

        @pl.when(me == n)
        def _():
            expect(1, group, 2)
            expect(f, group)

        @pl.when(me == f)
        def _():
            expect(h - 1, group, 3)

        @pl.when(jnp.logical_and(me != h, here != group))
        def _():
            expect(me, group)

    for y in range(n_tile):
        by_me = jnp.logical_or(heavy, y == me)
        total = None
        for d in range(1, n_sum):
            term = landed[y, lax.rem(here + d, n_sum)].astype(jnp.float32)
            total = term if total is None else total + term

        @pl.when(by_me)
        def _():
            out_ref[:, y * rows : (y + 1) * rows] = total + own[y, here]

        @pl.when(jnp.logical_not(by_me))
        def _():
            out_ref[:, y * rows : (y + 1) * rows] = total + landed[y, here].astype(jnp.float32)

    @pl.when(jnp.logical_not(heavy))
    def _():
        for piece in range(n_sum + 1):
            if piece != n_sum // 2:
                block_copy(me, piece).wait_send()
        drain(*diagonal_send)

    @pl.when(jnp.logical_or(me == far, me == twin))
    def _():
        block_copy(me, n_sum // 2).wait_send()

    @pl.when(heavy)
    def _():
        for message in (*twin_sends, near_send, *near_sends, far_send, *far_sends):
            drain(*message)


def line_kernel(n_tile, n_cone, n_rep, pattern_hbm, scale_hbm, values_hbm, point_hbm, out_ref,
           pattern_ref, scale_ref, values_ref, point_ref, load_sem, unit_ref, held, ids, part, landed, send_sem, recv_sem, part_send, part_recv):
    rows = values_ref.shape[0]
    cones, width = point_ref.shape
    n_sum = n_cone * n_rep
    strip = rows // n_sum
    me = lax.axis_index("tile")
    here = lax.axis_index("cone") * n_rep + lax.axis_index("rep")
    has_left, has_right = me > 0, me < n_tile - 1

    def peer(d):
        other = lax.rem(here + d, n_sum)
        return other, {"cone": other // n_rep, "rep": lax.rem(other, n_rep)}

    barrier = pltpu.get_barrier_semaphore()

    @pl.when(has_left)
    def _():
        pl.semaphore_signal(barrier, inc=1, device_id={"tile": me - 1}, device_id_type=MESH)

    @pl.when(has_right)
    def _():
        pl.semaphore_signal(barrier, inc=1, device_id={"tile": me + 1}, device_id_type=MESH)

    for d in range(1, n_sum):
        pl.semaphore_signal(barrier, inc=1, device_id=peer(d)[1], device_id_type=MESH)

    waits = load_all(
        (
            (pattern_hbm, pattern_ref),
            (scale_hbm, scale_ref),
            (point_hbm, point_ref),
            *(
                (values_hbm.at[pl.ds(q * strip, strip)], values_ref.at[pl.ds(q * strip, strip)])
                for q in range(n_sum)
            ),
        ),
        load_sem,
    )

    def block_copy(src, piece, right):
        ref = ids.at[src] if piece == n_sum else held.at[src, piece]
        return pltpu.make_async_remote_copy(
            src_ref=ref,
            dst_ref=ref,
            send_sem=send_sem.at[0 if right else 1, src, piece],
            recv_sem=recv_sem.at[src, piece],
            device_id={"tile": me + 1 if right else me - 1},
            device_id_type=MESH,
        )

    def send_own(piece):
        @pl.when(has_right)
        def _():
            block_copy(me, piece, True).start()

        @pl.when(has_left)
        def _():
            block_copy(me, piece, False).start()

    def on_ids():
        pl.semaphore_wait(
            barrier, has_left.astype(jnp.int32) + has_right.astype(jnp.int32) + (n_sum - 1)
        )
        send_own(n_sum)

    pack(pattern_ref, scale_ref, values_ref, point_ref, unit_ref, ids.at[me], held.at[me], waits, on_ids, send_own)

    def part_copy(src, d):
        other, device = peer(d)
        return pltpu.make_async_remote_copy(
            src_ref=part.at[src, other],
            dst_ref=landed.at[src, d - 1],
            send_sem=part_send.at[src, d - 1],
            recv_sem=part_recv.at[src, d - 1],
            device_id=device,
            device_id_type=MESH,
        )

    def product(src, own):
        left = wide(held.at[me]) if own else matched(held.at[me], ids[me], ids[src])
        block = outer(left, wide(held.at[src]))
        part[src] = block.reshape(n_sum, strip, width)
        for d in range(1, n_sum):
            part_copy(src, d).start()

    product(me, True)

    def step(s, carry):
        from_left, from_right = me - s, me + s
        for piece in (n_sum, *range(n_sum)):
            @pl.when(from_left >= 0)
            def _():
                block_copy(from_left, piece, True).wait_recv()

                @pl.when(has_right)
                def _():
                    block_copy(from_left, piece, True).start()

            @pl.when(from_right < n_tile)
            def _():
                block_copy(from_right, piece, False).wait_recv()

                @pl.when(has_left)
                def _():
                    block_copy(from_right, piece, False).start()

        @pl.when(from_left >= 0)
        def _():
            product(from_left, False)

        @pl.when(from_right < n_tile)
        def _():
            product(from_right, False)

        return carry

    lax.fori_loop(1, n_tile, step, 0)

    for src in range(n_tile):
        total = part[src, here]
        for d in range(1, n_sum):
            part_copy(src, d).wait_recv()
            total = total + landed[src, d - 1]
        out_ref[:, src * rows : (src + 1) * rows] = total

    def drain(src, carry):
        for d in range(1, n_sum):
            part_copy(src, d).wait_send()

        @pl.when(jnp.logical_and(has_right, src <= me))
        def _():
            for piece in range(n_sum + 1):
                block_copy(src, piece, True).wait_send()

        @pl.when(jnp.logical_and(has_left, src >= me))
        def _():
            for piece in range(n_sum + 1):
                block_copy(src, piece, False).wait_send()

        return carry

    lax.fori_loop(0, n_tile, drain, 0)


def solution(mesh):
    n_tile, n_cone, n_rep = mesh.shape["tile"], mesh.shape["cone"], mesh.shape["rep"]
    n_sum = n_cone * n_rep

    def per_device(values, pattern, cone_point, cone_scale):
        rows, cols = values.shape
        cones, width = cone_point.shape
        strip = rows // n_sum
        vmem = pl.BlockSpec(memory_space=pltpu.VMEM)
        hbm = pl.BlockSpec(memory_space=pltpu.HBM)
        loads = [
            pltpu.SMEM(pattern.shape, jnp.int32),
            pltpu.SMEM(cone_scale.shape, jnp.float32),
            pltpu.VMEM(values.shape, jnp.bfloat16),
            pltpu.VMEM((cones, width), jnp.float32),
            pltpu.SemaphoreType.DMA((3 + n_sum,)),
            pltpu.VMEM((cones, width), jnp.float32),
            pltpu.VMEM((n_tile, n_sum, SLOTS, strip, width), jnp.bfloat16),
            pltpu.VMEM((n_tile, 8, width), jnp.int32),
        ]
        if n_tile == 4 and n_rep == 2:
            body = functools.partial(middle_kernel, n_cone, n_rep)
            scratch = [
                pltpu.VMEM((n_tile, n_sum, strip, rows), jnp.float32),
                pltpu.VMEM((13, n_sum, strip, rows), PARTIAL),
                pltpu.VMEM((n_tile, n_sum, strip, rows), PARTIAL),
                pltpu.SemaphoreType.DMA((n_tile, n_sum + 1)),
                pltpu.SemaphoreType.DMA((n_tile, n_sum + 1)),
                pltpu.SemaphoreType.DMA((13, n_sum)),
                pltpu.SemaphoreType.DMA((n_tile, n_sum)),
                pltpu.SemaphoreType.REGULAR,
            ]
        else:
            body = functools.partial(line_kernel, n_tile, n_cone, n_rep)
            scratch = [
                pltpu.VMEM((n_tile, n_sum, strip, rows), jnp.float32),
                pltpu.VMEM((n_tile, n_sum - 1, strip, rows), jnp.float32),
                pltpu.SemaphoreType.DMA((2, n_tile, n_sum + 1)),
                pltpu.SemaphoreType.DMA((n_tile, n_sum + 1)),
                pltpu.SemaphoreType.DMA((n_tile, n_sum - 1)),
                pltpu.SemaphoreType.DMA((n_tile, n_sum - 1)),
            ]
        return pl.pallas_call(
            body,
            out_shape=pltpu.VMEM((strip, n_tile * rows), jnp.float32),
            in_specs=[hbm] * 4,
            out_specs=vmem,
            scratch_shapes=loads + scratch,
            compiler_params=pltpu.CompilerParams(
                collective_id=0, has_side_effects=True, vmem_limit_bytes=60 * 1024 * 1024
            ),
        )(pattern, cone_scale, values, cone_point)

    return jax.shard_map(
        per_device,
        mesh=mesh,
        in_specs=(
            P(("groups", "tile"), ("cone", "rep")),
            P(("groups", "tile"), ("cone", "rep")),
            P(("groups", "cone", "rep"), None),
            P(("groups", "cone", "rep")),
        ),
        out_specs=P(("groups", "tile", "cone", "rep"), None),
        check_vma=False,
    )
```

```python
import functools

import jax
import jax.numpy as jnp
from jax import lax
from jax.experimental import pallas as pl
from jax.experimental.pallas import tpu as pltpu
from jax.sharding import PartitionSpec as P

MESH = pl.DeviceIdType.MESH
SLOTS = 6


PARTIAL = jnp.bfloat16


def pack(pattern_ref, scale_ref, values_ref, point_ref, unit_ref, ids_me, held_me, waits, on_ids, on_strip):
    cones, width = point_ref.shape
    waits[0]()
    chosen = [[] for _ in range(SLOTS)]
    count = jnp.int32(0)
    for k in range(cones):
        live = pattern_ref[0, k]
        for s in range(SLOTS):
            chosen[s].append(live * (count == s).astype(jnp.int32) if k >= s else None)
        count = count + live
    for s in range(SLOTS):
        name = sum(chosen[s][k] * (k + 1) for k in range(s, cones))
        ids_me[s : s + 1, :] = jnp.full((1, width), name, jnp.int32)
    on_ids()
    waits[2]()
    lane = lax.broadcasted_iota(jnp.int32, (1, width), 1)
    signs = jnp.where(lane == 0, 1.0, -1.0).astype(jnp.float32)
    point = point_ref[...]
    det = jnp.sum(point * point * signs, axis=1, keepdims=True)
    unit_ref[...] = point / jnp.sqrt(det)
    waits[1]()
    slots = []
    for s in range(SLOTS):
        factor, unit, masks = 0.0, 0.0, []
        for k in range(s, cones):
            weight = chosen[s][k].astype(jnp.float32)
            factor = factor + weight * scale_ref[k]
            unit = unit + weight * unit_ref[k : k + 1, :]
            masks.append(jnp.full((1, width), weight, jnp.float32).astype(jnp.bfloat16))
        slots.append((factor, unit, masks))
    strip = held_me.shape[2]
    for q in range(held_me.shape[0]):
        waits[3 + q]()
        for s, (factor, unit, masks) in enumerate(slots):
            packed = None
            for k, mask in zip(range(s, cones), masks):
                term = values_ref[q * strip : (q + 1) * strip, k * width : (k + 1) * width] * mask
                packed = term if packed is None else packed + term
            tile = packed.astype(jnp.float32)
            proj = jnp.sum(tile * unit, axis=1, keepdims=True)
            held_me[q, s] = (factor * (2.0 * proj * unit - tile * signs)).astype(jnp.bfloat16)
        on_strip(q)


def load_all(pairs, load_sem):
    loads = [
        pltpu.make_async_copy(src, dst, load_sem.at[i]) for i, (src, dst) in enumerate(pairs)
    ]
    for load in loads:
        load.start()
    return [load.wait for load in loads]


def slots_of(ref):
    return [ref[:, s].reshape(-1, ref.shape[3]) for s in range(SLOTS)]


def wide(ref):
    return jnp.concatenate(slots_of(ref), axis=1)


def matched(first, first_ids, second_ids):
    moved = []
    tiles = slots_of(first)
    for b in range(SLOTS):
        total = None
        for a in range(SLOTS):
            same = (first_ids[a : a + 1, :] == second_ids[b : b + 1, :]).astype(jnp.float32)
            term = tiles[a] * same.astype(jnp.bfloat16)
            total = term if total is None else total + term
        moved.append(total)
    return jnp.concatenate(moved, axis=1)


def outer(x, y):
    return lax.dot_general(
        x, y, (((1,), (1,)), ((), ())), preferred_element_type=jnp.float32
    )


def middle_kernel(n_cone, n_rep, pattern_hbm, scale_hbm, values_hbm, point_hbm, out_ref,
                  pattern_ref, scale_ref, values_ref, point_ref, load_sem, unit_ref, held, ids,
                  own, part, landed, send_sem, recv_sem, part_send, part_recv, turn):
    n_tile = 4
    rows, width = values_ref.shape[0], point_ref.shape[1]
    n_sum = n_cone * n_rep
    strip = rows // n_sum
    me, rep = lax.axis_index("tile"), lax.axis_index("rep")
    here = lax.axis_index("cone") * n_rep + rep
    heavy_tile = 1 + rep
    heavy = me == heavy_tile
    twin = 3 - heavy_tile
    near = 3 * rep
    far = 3 - near

    waits = load_all(
        (
            (pattern_hbm, pattern_ref),
            (scale_hbm, scale_ref),
            (point_hbm, point_ref),
            *(
                (values_hbm.at[pl.ds(q * strip, strip)], values_ref.at[pl.ds(q * strip, strip)])
                for q in range(n_sum)
            ),
        ),
        load_sem,
    )

    def place(tile, group):
        return {"tile": tile, "cone": group // n_rep, "rep": lax.rem(group, n_rep)}

    barrier = pltpu.get_barrier_semaphore()
    everyone = n_tile * n_sum
    for d in range(1, everyone):
        other = lax.rem(me * n_sum + here + d, everyone)
        pl.semaphore_signal(
            barrier, inc=1, device_id=place(other // n_sum, lax.rem(other, n_sum)), device_id_type=MESH
        )

    def block_copy(src, piece):
        ref = ids.at[src] if piece == n_sum else held.at[src, piece]
        return pltpu.make_async_remote_copy(
            src_ref=ref,
            dst_ref=ref,
            send_sem=send_sem.at[src, piece],
            recv_sem=recv_sem.at[src, piece],
            device_id={"tile": heavy_tile},
            device_id_type=MESH,
        )

    def send_own(piece):
        @pl.when(jnp.logical_not(heavy) if piece == n_sum else jnp.logical_or(me == near, me == twin))
        def _():
            block_copy(me, piece).start()

    def on_ids():
        pl.semaphore_wait(barrier, everyone - 1)
        send_own(n_sum)

    pack(pattern_ref, scale_ref, values_ref, point_ref, unit_ref, ids.at[me], held.at[me], waits, on_ids, send_own)

    @pl.when(me == near)
    def _():
        block_copy(me, n_sum // 2).wait_send()
        pl.semaphore_signal(turn, inc=1, device_id={"rep": 1 - rep}, device_id_type=MESH)

    @pl.when(me == far)
    def _():
        pl.semaphore_wait(turn, 1)
        for piece in range(n_sum):
            block_copy(me, piece).start()

    def strip_copy(slot, x, y, group, count=1):
        return pltpu.make_async_remote_copy(
            src_ref=part.at[pl.ds(slot, count), group],
            dst_ref=landed.at[pl.ds(y, count), here],
            send_sem=part_send.at[slot, group],
            recv_sem=part_recv.at[y, here],
            device_id=place(x, group),
            device_id_type=MESH,
        )

    def send(slot, x, y, mine, count=1):
        for d in range(1 if mine else 0, n_sum):
            strip_copy(slot, x, y, lax.rem(here + d, n_sum), count).start()

    def drain(slot, x, y, mine, count=1):
        for d in range(1 if mine else 0, n_sum):
            strip_copy(slot, x, y, lax.rem(here + d, n_sum), count).wait_send()

    def put(slot, block, y=None):
        strips = block.reshape(n_sum, strip, width)
        part[slot] = strips.astype(PARTIAL)
        if y is not None:
            own[y] = strips

    def arrive(src, piece):
        block_copy(src, piece).wait_recv()

    def moved(blocks, to):
        return jnp.concatenate([matched(held.at[x], ids[x], ids[to]) for x in blocks], axis=0)

    low = heavy_tile - 1
    diagonal_send = (0, me, me, True, 1)
    twin_sends = ((0, me, 1, True, 2), (2, twin, me, False, 1))
    near_send = (4, near, 1, False, 2)
    near_sends = ((3, twin, near, False, 1), (7, me, near, True, 1))
    far_send = (9, far, low, False, 3)
    far_sends = ((6, near, far, False, 1), (12, twin, far, False, 1), (8, me, far, True, 1))

    put(jnp.where(heavy, low, 0), outer(wide(held.at[me]), wide(held.at[me])), me)

    @pl.when(jnp.logical_not(heavy))
    def _():
        send(*diagonal_send)

    @pl.when(heavy)
    def _():
        for piece in (n_sum, *range(n_sum)):
            arrive(twin, piece)
        left, right = moved((me,), twin), wide(held.at[twin])
        put(2, outer(right, left))
        put(twin - 1, outer(left, right), twin)
        for message in twin_sends:
            send(*message)

        arrive(near, n_sum)
        left = moved((me, twin), near)
        for q in range(n_sum):
            arrive(near, q)
        right = wide(held.at[near])
        block = outer(right, left)
        put(4 + me - 1, block[:, :width])
        put(4 + twin - 1, block[:, width:])
        send(*near_send)
        block = outer(left, right)
        put(7, block[:rows], near)
        put(3, block[rows:])
        for message in near_sends:
            send(*message)

        arrive(far, n_sum)
        left = moved((me, near, twin), far)
        half = n_sum // 2
        for first in (0, half):
            for q in range(first, first + half):
                arrive(far, q)
            block = outer(wide(held.at[far, pl.ds(first, half)]), left).astype(PARTIAL)
            for i, x in enumerate((me, near, twin)):
                part[9 + x - low, pl.ds(first, half)] = block[:, i * width : (i + 1) * width].reshape(half, strip, width)
            for q in range(first, first + half):
                strip_copy(9, far, low, q, 3).start()
        block = outer(left, wide(held.at[far]))
        put(8, block[:rows], far)
        put(6, block[rows : 2 * rows])
        put(12, block[2 * rows :])
        for message in far_sends:
            send(*message)

    def expect(y, group, count=1):
        pltpu.make_async_remote_copy(
            src_ref=part.at[pl.ds(0, count), 0],
            dst_ref=landed.at[pl.ds(y, count), group],
            send_sem=part_send.at[0, 0],
            recv_sem=part_recv.at[y, group],
            device_id=place(lax.rem(me + 1, n_tile), group),
            device_id_type=MESH,
        ).wait_recv()

    for group in range(n_sum):
        h, n = 1 + group % n_rep, 3 * (group % n_rep)
        l, f = 3 - h, 3 - n

        @pl.when(jnp.logical_and(me == h, here != group))
        def _():
            expect(1, group, 2)
            expect(n, group)
            expect(f, group)

        @pl.when(me == l)
        def _():
            expect(h, group)
            expect(n, group)
            expect(f, group)

        @pl.when(me == n)
        def _():
            expect(1, group, 2)
            expect(f, group)

        @pl.when(me == f)
        def _():
            expect(h - 1, group, 3)

        @pl.when(jnp.logical_and(me != h, here != group))
        def _():
            expect(me, group)

    for y in range(n_tile):
        by_me = jnp.logical_or(heavy, y == me)
        total = None
        for d in range(1, n_sum):
            term = landed[y, lax.rem(here + d, n_sum)].astype(jnp.float32)
            total = term if total is None else total + term

        @pl.when(by_me)
        def _():
            out_ref[:, y * rows : (y + 1) * rows] = total + own[y, here]

        @pl.when(jnp.logical_not(by_me))
        def _():
            out_ref[:, y * rows : (y + 1) * rows] = total + landed[y, here].astype(jnp.float32)

    @pl.when(jnp.logical_not(heavy))
    def _():
        for piece in range(n_sum + 1):
            if piece != n_sum // 2:
                block_copy(me, piece).wait_send()
        drain(*diagonal_send)

    @pl.when(jnp.logical_or(me == far, me == twin))
    def _():
        block_copy(me, n_sum // 2).wait_send()

    @pl.when(heavy)
    def _():
        for message in (*twin_sends, near_send, *near_sends, far_send, *far_sends):
            drain(*message)


def line_kernel(n_tile, n_cone, n_rep, pattern_hbm, scale_hbm, values_hbm, point_hbm, out_ref,
           pattern_ref, scale_ref, values_ref, point_ref, load_sem, unit_ref, held, ids, part, landed, send_sem, recv_sem, part_send, part_recv):
    rows = values_ref.shape[0]
    cones, width = point_ref.shape
    n_sum = n_cone * n_rep
    strip = rows // n_sum
    me = lax.axis_index("tile")
    here = lax.axis_index("cone") * n_rep + lax.axis_index("rep")
    has_left, has_right = me > 0, me < n_tile - 1

    def peer(d):
        other = lax.rem(here + d, n_sum)
        return other, {"cone": other // n_rep, "rep": lax.rem(other, n_rep)}

    barrier = pltpu.get_barrier_semaphore()

    @pl.when(has_left)
    def _():
        pl.semaphore_signal(barrier, inc=1, device_id={"tile": me - 1}, device_id_type=MESH)

    @pl.when(has_right)
    def _():
        pl.semaphore_signal(barrier, inc=1, device_id={"tile": me + 1}, device_id_type=MESH)

    for d in range(1, n_sum):
        pl.semaphore_signal(barrier, inc=1, device_id=peer(d)[1], device_id_type=MESH)

    waits = load_all(
        (
            (pattern_hbm, pattern_ref),
            (scale_hbm, scale_ref),
            (point_hbm, point_ref),
            *(
                (values_hbm.at[pl.ds(q * strip, strip)], values_ref.at[pl.ds(q * strip, strip)])
                for q in range(n_sum)
            ),
        ),
        load_sem,
    )

    def block_copy(src, piece, right):
        ref = ids.at[src] if piece == n_sum else held.at[src, piece]
        return pltpu.make_async_remote_copy(
            src_ref=ref,
            dst_ref=ref,
            send_sem=send_sem.at[0 if right else 1, src, piece],
            recv_sem=recv_sem.at[src, piece],
            device_id={"tile": me + 1 if right else me - 1},
            device_id_type=MESH,
        )

    def send_own(piece):
        @pl.when(has_right)
        def _():
            block_copy(me, piece, True).start()

        @pl.when(has_left)
        def _():
            block_copy(me, piece, False).start()

    def on_ids():
        pl.semaphore_wait(
            barrier, has_left.astype(jnp.int32) + has_right.astype(jnp.int32) + (n_sum - 1)
        )
        send_own(n_sum)

    pack(pattern_ref, scale_ref, values_ref, point_ref, unit_ref, ids.at[me], held.at[me], waits, on_ids, send_own)

    def part_copy(src, d):
        other, device = peer(d)
        return pltpu.make_async_remote_copy(
            src_ref=part.at[src, other],
            dst_ref=landed.at[src, d - 1],
            send_sem=part_send.at[src, d - 1],
            recv_sem=part_recv.at[src, d - 1],
            device_id=device,
            device_id_type=MESH,
        )

    def product(src, own):
        left = wide(held.at[me]) if own else matched(held.at[me], ids[me], ids[src])
        block = outer(left, wide(held.at[src]))
        part[src] = block.reshape(n_sum, strip, width)
        for d in range(1, n_sum):
            part_copy(src, d).start()

    product(me, True)

    def step(s, carry):
        from_left, from_right = me - s, me + s
        for piece in (n_sum, *range(n_sum)):
            @pl.when(from_left >= 0)
            def _():
                block_copy(from_left, piece, True).wait_recv()

                @pl.when(has_right)
                def _():
                    block_copy(from_left, piece, True).start()

            @pl.when(from_right < n_tile)
            def _():
                block_copy(from_right, piece, False).wait_recv()

                @pl.when(has_left)
                def _():
                    block_copy(from_right, piece, False).start()

        @pl.when(from_left >= 0)
        def _():
            product(from_left, False)

        @pl.when(from_right < n_tile)
        def _():
            product(from_right, False)

        return carry

    lax.fori_loop(1, n_tile, step, 0)

    for src in range(n_tile):
        total = part[src, here]
        for d in range(1, n_sum):
            part_copy(src, d).wait_recv()
            total = total + landed[src, d - 1]
        out_ref[:, src * rows : (src + 1) * rows] = total

    def drain(src, carry):
        for d in range(1, n_sum):
            part_copy(src, d).wait_send()

        @pl.when(jnp.logical_and(has_right, src <= me))
        def _():
            for piece in range(n_sum + 1):
                block_copy(src, piece, True).wait_send()

        @pl.when(jnp.logical_and(has_left, src >= me))
        def _():
            for piece in range(n_sum + 1):
                block_copy(src, piece, False).wait_send()

        return carry

    lax.fori_loop(0, n_tile, drain, 0)


def solution(mesh):
    n_tile, n_cone, n_rep = mesh.shape["tile"], mesh.shape["cone"], mesh.shape["rep"]
    n_sum = n_cone * n_rep

    def per_device(values, pattern, cone_point, cone_scale):
        rows, cols = values.shape
        cones, width = cone_point.shape
        strip = rows // n_sum
        vmem = pl.BlockSpec(memory_space=pltpu.VMEM)
        hbm = pl.BlockSpec(memory_space=pltpu.HBM)
        loads = [
            pltpu.SMEM(pattern.shape, jnp.int32),
            pltpu.SMEM(cone_scale.shape, jnp.float32),
            pltpu.VMEM(values.shape, jnp.bfloat16),
            pltpu.VMEM((cones, width), jnp.float32),
            pltpu.SemaphoreType.DMA((3 + n_sum,)),
            pltpu.VMEM((cones, width), jnp.float32),
            pltpu.VMEM((n_tile, n_sum, SLOTS, strip, width), jnp.bfloat16),
            pltpu.VMEM((n_tile, 8, width), jnp.int32),
        ]
        if n_tile == 4 and n_rep == 2:
            body = functools.partial(middle_kernel, n_cone, n_rep)
            scratch = [
                pltpu.VMEM((n_tile, n_sum, strip, rows), jnp.float32),
                pltpu.VMEM((13, n_sum, strip, rows), PARTIAL),
                pltpu.VMEM((n_tile, n_sum, strip, rows), PARTIAL),
                pltpu.SemaphoreType.DMA((n_tile, n_sum + 1)),
                pltpu.SemaphoreType.DMA((n_tile, n_sum + 1)),
                pltpu.SemaphoreType.DMA((13, n_sum)),
                pltpu.SemaphoreType.DMA((n_tile, n_sum)),
                pltpu.SemaphoreType.REGULAR,
            ]
        else:
            body = functools.partial(line_kernel, n_tile, n_cone, n_rep)
            scratch = [
                pltpu.VMEM((n_tile, n_sum, strip, rows), jnp.float32),
                pltpu.VMEM((n_tile, n_sum - 1, strip, rows), jnp.float32),
                pltpu.SemaphoreType.DMA((2, n_tile, n_sum + 1)),
                pltpu.SemaphoreType.DMA((n_tile, n_sum + 1)),
                pltpu.SemaphoreType.DMA((n_tile, n_sum - 1)),
                pltpu.SemaphoreType.DMA((n_tile, n_sum - 1)),
            ]
        return pl.pallas_call(
            body,
            out_shape=pltpu.VMEM((strip, n_tile * rows), jnp.float32),
            in_specs=[hbm] * 4,
            out_specs=vmem,
            scratch_shapes=loads + scratch,
            compiler_params=pltpu.CompilerParams(
                collective_id=0, has_side_effects=True, vmem_limit_bytes=60 * 1024 * 1024
            ),
        )(pattern, cone_scale, values, cone_point)

    return jax.shard_map(
        per_device,
        mesh=mesh,
        in_specs=(
            P(("groups", "tile"), ("cone", "rep")),
            P(("groups", "tile"), ("cone", "rep")),
            P(("groups", "cone", "rep"), None),
            P(("groups", "cone", "rep")),
        ),
        out_specs=P(("groups", "tile", "cone", "rep"), None),
        check_vma=False,
    )
```
